512 devices in a mesh: tm: 16 (over y, z_hi, core), space: 32 (over z_lo, x).
Axes of the slice: x: 4, y: 4, z: 16 (z_hi: 2, z_lo: 8; z = z_hi * 8 + z_lo), core: 2. Of those that a mesh axis runs over, the one named last changes fastest.
Arguments:
- phase_guess: float32 [16, 128, 32, 512], P('tm', 'space'), may hold values from -1 to 1
- solute_guess: float32 [16, 128, 32, 512], P('tm', 'space'), may hold values from -0.9 to 0.3
- solute_start: float32 [128, 32, 512], P('space'), may hold values from -0.8 to 0
- nuclei: int32 [8, 3], replicated, may hold values from 0 to 511, as said below
Outputs:
- phase_next: float32 [16, 128, 32, 512], P('tm', 'space')
- solute_next: float32 [16, 128, 32, 512], P('tm', 'space')
The draws below stay inside these ranges and needn't reach their ends.
Inputs may be any that keep to these rules, and one draw needn't show every extreme that they name: `nuclei`: column 0 lies in 0 .. 127, column 1 in 0 .. 31, column 2 in 0 .. 511.
All inputs are finite; a program needn't handle non-finite values.
Results may differ from the reference program's by a relative error of at most 0.00002.
Values sent between devices are 32-bit elements; how exact they have to be, the bound alone decides.
No kernel may reach another device: no remote copies, remote signals or barrier semaphores. Data moves between devices by JAX's collectives and lax.ppermute only.
A program may use at most 64 MiB of HBM per device.

```python
import jax
import jax.numpy as jnp

NY = 512
NZ = 32
M = 4
NSEEDS = 8
NX = 128
BLOCKS = 16


def draw_nuclei(key, part):
    key = jax.random.fold_in(key, 7)
    key_x, key_z, key_y = jax.random.split(key, 3)
    first = jax.random.randint(key_x, (NSEEDS,), 0, NX)
    middle = jax.random.randint(key_z, (NSEEDS,), 0, NZ)
    last = jax.random.randint(key_y, (NSEEDS,), 0, NY)
    first = first.at[0].set(NX - 1).at[1].set(0)
    last = last.at[0].set(NY - 1).at[1].set(0)
    return jnp.stack([first, middle, last], axis=1).astype(jnp.int32)


def level_of(rng, extent, shards, smallest, top_value):
    loudness = 1.0
    for dim, blocks in shards:
        draws = jax.random.uniform(jax.random.fold_in(jax.random.fold_in(rng, 6), dim), (blocks,), jnp.float32, smallest / len(shards), top_value / len(shards))
        loudness = loudness * jnp.repeat(jnp.exp(draws), extent[dim] // blocks).reshape((-1,) + (1,) * (len(extent) - 1 - dim))
    return loudness


def setup_inputs(seed: int = 0) -> dict:
    key_of = jax.random.split(jax.random.key(seed), 5)
    phase_guess = jnp.clip(jax.random.uniform(key_of[0], (BLOCKS, NX, NZ, NY), jnp.float32, -1.0, 1.0) * level_of(key_of[0], (BLOCKS, NX, NZ, NY), ((0, 16), (1, 32)), -0.4, 0.0), -1.0, 1.0)
    solute_guess = jnp.clip(-0.9 + 1.2 * jax.random.uniform(key_of[1], (BLOCKS, NX, NZ, NY), jnp.float32) ** level_of(key_of[1], (BLOCKS, NX, NZ, NY), ((0, 16), (1, 32)), -0.2, 0.2), -0.9, 0.3)
    solute_start = jnp.clip(-0.8 + 0.8 * jax.random.uniform(key_of[2], (NX, NZ, NY), jnp.float32) ** level_of(key_of[2], (NX, NZ, NY), ((0, 32),), -0.2, 0.2), -0.8, 0.0)
    nuclei = draw_nuclei(jax.random.fold_in(key_of[4], 71), 0)
    return {"phase_guess": phase_guess, "solute_guess": solute_guess, "solute_start": solute_start, "nuclei": nuclei}


FINE_RATE = 0.025
DIFFUSION = 1.5
COUPLING = 2.0
ANISO = 0.05
GRAD_FLOOR = 0.01
WIDTH_SQ = 18.0


def step_core(extended, rate):
    phase = extended[0]
    solute = extended[1]
    phase_mid = phase[1:-1]
    solute_mid = solute[1:-1]

    def laplacian(full, centre):
        zpad = jnp.concatenate([centre[:, :1], centre, centre[:, -1:]], axis=1)
        total = full[2:] + full[:-2] + jnp.roll(centre, 1, 2) + jnp.roll(centre, -1, 2)
        return total + zpad[:, 2:] + zpad[:, :-2] - 6.0 * centre

    zphase = jnp.concatenate([phase_mid[:, :1], phase_mid, phase_mid[:, -1:]], axis=1)
    grad_x = 0.5 * (phase[2:] - phase[:-2])
    grad_y = 0.5 * (jnp.roll(phase_mid, -1, 2) - jnp.roll(phase_mid, 1, 2))
    grad_z = 0.5 * (zphase[:, 2:] - zphase[:, :-2])
    squared = grad_x * grad_x + grad_y * grad_y + grad_z * grad_z
    quartic = (grad_x ** 4 + grad_y ** 4 + grad_z ** 4) / jnp.maximum(squared, GRAD_FLOOR) ** 2
    aniso = 1.0 + ANISO * (4.0 * quartic - 3.0)
    wetness = 1.0 - phase_mid * phase_mid
    phase_new = phase_mid + rate * (aniso * aniso * laplacian(phase, phase_mid) + phase_mid - phase_mid ** 3 - COUPLING * solute_mid * wetness * wetness)
    solute_new = solute_mid + rate * DIFFUSION * laplacian(solute, solute_mid) + 0.5 * (phase_new - phase_mid)
    return jnp.stack([phase_new, solute_new])


def whole_step(state, rate):
    extended = jnp.concatenate([state[:, -1:], state, state[:, :1]], axis=1)
    return step_core(extended, rate)


def nucleus_phase(xs, zs, ys, nuclei, nx_total, ny_total):
    best = jnp.zeros((xs.shape[0], zs.shape[0], ys.shape[0]), jnp.float32)
    for nucleus in range(NSEEDS):
        dist_x = jnp.abs(xs - nuclei[nucleus, 0])
        dist_x = jnp.minimum(dist_x, nx_total - dist_x)
        dist_y = jnp.abs(ys - nuclei[nucleus, 2])
        dist_y = jnp.minimum(dist_y, ny_total - dist_y)
        dist_z = zs - nuclei[nucleus, 1]
        dist_sq = (dist_x * dist_x)[:, None, None] + (dist_z * dist_z)[None, :, None] + (dist_y * dist_y)[None, None, :]
        best = jnp.maximum(best, jnp.exp(-dist_sq.astype(jnp.float32) / WIDTH_SQ))
    return 2.0 * best - 1.0


def reference(phase_guess, solute_guess, solute_start, nuclei):
    xs = jnp.arange(NX, dtype=jnp.int32)
    zs = jnp.arange(NZ, dtype=jnp.int32)
    ys = jnp.arange(NY, dtype=jnp.int32)
    initial = jnp.stack([nucleus_phase(xs, zs, ys, nuclei, NX, NY), solute_start])
    coarse_rate = M * FINE_RATE
    corrections = []
    for block in range(BLOCKS - 1):
        if block == 0:
            start = initial
        else:
            start = jnp.stack([phase_guess[block], solute_guess[block]])
        fine = start
        for turn in range(M):
            fine = whole_step(fine, FINE_RATE)
        corrections.append(fine - whole_step(start, coarse_rate))
    values = [initial]
    current = initial
    for block in range(BLOCKS - 1):
        current = whole_step(current, coarse_rate) + corrections[block]
        values.append(current)
    stacked = jnp.stack(values)
    return stacked[:, 0], stacked[:, 1]
```

```python
import jax
import jax.numpy as jnp
from jax import lax
from jax.experimental import pallas as pl
from jax.experimental.pallas import tpu as pltpu
from jax.sharding import PartitionSpec as P

M = 4
FINE_RATE = 0.025
COARSE_RATE = M * FINE_RATE
DIFFUSION = 1.5
WIDTH_SQ = 18.0
AXES = ("tm", "space")


def device(x, y, z_lo, z_hi, core):
    return (y * 4 + z_hi * 2 + core) * 32 + z_lo * 4 + x


def ring_of(x, y, core):
    return 2 * (y * 4 + (3 - x if y & 1 else x)) + core


def place(ring):
    q, core = ring >> 1, ring & 1
    y, x = q >> 2, q & 3
    return (3 - x if y & 1 else x), y, core


PLANES = [(z_lo, z_hi) for z_hi in range(2) for z_lo in range(8)]


def on_ring(ring, plane):
    x, y, core = place(ring % 32)
    return device(x, y, plane[0], plane[1], core)


PLANE_GROUPS = [[on_ring(i, plane) for i in range(32)] for plane in PLANES]
RIGHT = [(on_ring(i, plane), on_ring(i + 1, plane)) for plane in PLANES for i in range(32)]
LEFT = [(b, a) for a, b in RIGHT]
ACROSS = [(i, i ^ 2) for i in range(16)]


def row_pairs(parity):
    pairs = []
    for z_lo in range(parity, 8, 2):
        for i in range(32):
            for z_hi in range(2):
                a, b = on_ring(i, (z_lo, z_hi)), on_ring(i, ((z_lo + 1) % 8, z_hi))
                pairs += [(a, b), (b, a)]
    return pairs


def space_pairs(parity):
    pairs = []
    for s in range(parity, 32, 2):
        pairs += [(s, (s + 1) % 32), ((s + 1) % 32, s)]
    return pairs


def growth(pc, uc, pxm, pxp, pym, pyp, pzm, pzp):
    dx, dy, dz = pxp - pxm, pyp - pym, pzp - pzm
    dx, dy, dz = dx * dx, dy * dy, dz * dz
    floor = jnp.maximum(dx + dy + dz, 0.04)
    quartic = (dx * dx + dy * dy + dz * dz) / (floor * floor)
    aniso = 0.85 + 0.2 * quartic
    lap = ((pxp + pxm) + (pyp + pym)) + (pzp + pzm) - 6.0 * pc
    wet = 1.0 - pc * pc
    return aniso * aniso * lap + wet * (pc - 2.0 * uc * wet)


def block_index():
    return lax.axis_index("tm"), lax.axis_index("space")


def start_kernel(nuclei, p_in, u_in, u_start, out):
    tm, space = block_index()

    @pl.when(tm != 0)
    def _():
        out[0] = p_in[0]
        out[1] = u_in[0]

    @pl.when(tm == 0)
    def _():
        zs = lax.broadcasted_iota(jnp.int32, (8, 512), 0)
        ys = lax.broadcasted_iota(jnp.int32, (8, 512), 1)
        for g in range(4):
            sides = []
            for n in range(8):
                dy = jnp.abs(ys - nuclei[n, 2])
                dy = jnp.minimum(dy, 512 - dy)
                dz = zs + 8 * g - nuclei[n, 1]
                sides.append(dy * dy + dz * dz)
            for r in range(4):
                best = None
                for n in range(8):
                    dx = jnp.abs(space * 4 + r - nuclei[n, 0])
                    dx = jnp.minimum(dx, 128 - dx)
                    here = sides[n] + dx * dx
                    best = here if best is None else jnp.minimum(best, here)
                b = jnp.exp(-best.astype(jnp.float32) / WIDTH_SQ)
                out[0, r, 8 * g : 8 * g + 8, :] = 2.0 * b - 1.0
        out[1] = u_start[...]


def transpose_lanes(parts):
    slot = lax.broadcasted_iota(jnp.int32, (8, 128), 1) // 16
    parts = list(parts)
    for d in (4, 2, 1):
        low = (slot & d) == 0
        for a in range(8):
            if not a & d:
                top, bottom = parts[a], parts[a + d]
                parts[a] = jnp.where(low, top, pltpu.roll(bottom, 16 * d, 1))
                parts[a + d] = jnp.where(low, pltpu.roll(top, 128 - 16 * d, 1), bottom)
    return parts


def relax_kernel(start, odd, even, out, one, two, coarse):
    tm, space = block_index()
    keep = jnp.where(tm == 0, 0.0, 1.0)

    def put(buf, f, row, g, value):
        buf[f, row, 8 + 8 * g : 16 + 8 * g, :] = value
        if g == 0:
            buf[f, row, 7:8, :] = value[0:1]
        if g == 3:
            buf[f, row, 40:41, :] = value[7:8]

    def fill(before, after):
        for f in range(2):
            for part, src in enumerate((before, start, after)):
                for r in range(4):
                    for g in range(4):
                        put(one, f, 4 * part + r, g, src[f, r, 8 * g : 8 * g + 8, :])

    @pl.when(space % 2 == 0)
    def _():
        fill(odd, even)

    @pl.when(space % 2 == 1)
    def _():
        fill(even, odd)

    def one_row(src, dst, row, first):
        for g in range(4):
            at = slice(8 + 8 * g, 16 + 8 * g)
            up = slice(9 + 8 * g, 17 + 8 * g)
            down = slice(7 + 8 * g, 15 + 8 * g)
            pc, uc = src[0, row, at, :], src[1, row, at, :]
            rate = growth(
                pc, uc,
                src[0, row - 1, at, :], src[0, row + 1, at, :],
                pltpu.roll(pc, 1, 1), pltpu.roll(pc, 511, 1),
                src[0, row, down, :], src[0, row, up, :],
            )
            ulap = (
                (src[1, row - 1, at, :] + src[1, row + 1, at, :])
                + (pltpu.roll(uc, 1, 1) + pltpu.roll(uc, 511, 1))
                + (src[1, row, down, :] + src[1, row, up, :])
                - 6.0 * uc
            )
            gain = FINE_RATE * rate
            put(dst, 0, row, g, pc + gain)
            put(dst, 1, row, g, uc + (FINE_RATE * DIFFUSION) * ulap + 0.5 * gain)
            if first:
                gain = COARSE_RATE * rate
                coarse[0, row - 4, 8 * g : 8 * g + 8, :] = pc + gain
                coarse[1, row - 4, 8 * g : 8 * g + 8, :] = (
                    uc + (COARSE_RATE * DIFFUSION) * ulap + 0.5 * gain
                )

    def sweep(src, dst, lo, hi, first=False):
        @pl.loop(lo, hi)
        def _(row):
            one_row(src, dst, row, first)

    sweep(one, two, 1, 4)
    sweep(one, two, 4, 8, True)
    sweep(one, two, 8, 11)
    sweep(two, one, 2, 10)
    sweep(one, two, 3, 9)
    sweep(two, one, 4, 8)

    for f in range(2):
        for rp in range(2):
            for b in range(4):
                parts = []
                for g in range(4):
                    for rr in range(2):
                        r = 2 * rp + rr
                        lanes = slice(128 * b, 128 * b + 128)
                        fine = one[f, 4 + r, 8 + 8 * g : 16 + 8 * g, lanes]
                        parts.append(fine - keep * coarse[f, r, 8 * g : 8 * g + 8, lanes])
                for j, part in enumerate(transpose_lanes(parts)):
                    out[8 * b + j, f, rp] = part


HALO_PAIRS = (4, 3, 3, 2, 2, 1, 1, 0)
PAIR_AT = (0, 4, 7, 10, 12, 14, 15, 16)
QUADS = (8, 7, 7, 6, 6, 5, 5)
QUAD_AT = (0, 8, 15, 22, 28, 34, 39)


def lane32():
    return lax.broadcasted_iota(jnp.int32, (8, 128), 1) % 32


def piece_of(phase, own, other, first, z_hi):
    def get(slot, f, pair):
        if slot == 0 and first is not None:
            return first[f, pair]
        k = slot + 7 * phase
        x, y, core = pair // 2, k >> 2, k & 1
        i = ring_of(x, y, core) - 16 * phase
        mine = ((k >> 1) & 1) == z_hi
        return jnp.where(mine, own[i, f, pair % 2], other[i, f, pair % 2])

    return get


def edges_kernel(phase, *refs):
    if phase == 0:
        own, other, odd, even = refs
        first = None
    else:
        own, other, first, odd, even = refs
    tm, space = block_index()
    get = piece_of(phase, own, other, first, (tm // 2) % 2)
    z_odd = (space // 4) % 2 == 1
    for slot in range(7):
        n = HALO_PAIRS[slot]
        for f in range(2):
            for m in range(n):
                top, bottom = get(slot, f, m), get(slot, f, 8 - n + m)
                odd[PAIR_AT[slot] + m, f] = jnp.where(z_odd, bottom, top)
                even[PAIR_AT[slot] + m, f] = jnp.where(z_odd, top, bottom)


def rows_of(get, odd, even, z_odd, slot, f):
    n = HALO_PAIRS[slot]
    pieces = []
    for m in range(n):
        at = PAIR_AT[slot] + m
        pieces.append(jnp.where(z_odd, even[at, f], odd[at, f]))
    pieces += [get(slot, f, pair) for pair in range(8)]
    for m in range(n):
        at = PAIR_AT[slot] + m
        pieces.append(jnp.where(z_odd, odd[at, f], even[at, f]))
    rows = []
    for piece in pieces:
        rows += [pltpu.roll(piece, 8, 1), pltpu.roll(piece, 120, 1)]
    return rows


def lanes_kernel(phase, *refs):
    if phase == 0:
        own, other, odd, even, right, left = refs
        first = None
    else:
        own, other, first, odd, even, right, left = refs
    tm, space = block_index()
    get = piece_of(phase, own, other, first, (tm // 2) % 2)
    z_odd = (space // 4) % 2 == 1
    part = lane32() // 8
    for slot in range(7):
        for f in range(2):
            rows = rows_of(get, odd, even, z_odd, slot, f)
            for a in range(QUADS[slot]):
                r_edge = l_edge = None
                for q in range(4):
                    row = rows[4 * a + q]
                    r_part = pltpu.roll(row, (8 * q - 16) % 128, 1) if q != 2 else row
                    l_part = pltpu.roll(row, (8 * q - 8) % 128, 1) if q != 1 else row
                    if q == 0:
                        r_edge, l_edge = r_part, l_part
                    else:
                        r_edge = jnp.where(part == q, r_part, r_edge)
                        l_edge = jnp.where(part == q, l_part, l_edge)
                right[QUAD_AT[slot] + a, f] = r_edge
                left[QUAD_AT[slot] + a, f] = l_edge


def chain_kernel(phase, *refs):
    if phase == 0:
        own, other, odd, even, from_left, from_right, out, last, state, taus = refs
        first = before = None
    else:
        own, other, first, odd, even, from_left, from_right, before, out, state, taus = refs
    tm, space = block_index()
    z_hi = (tm // 2) % 2
    get = piece_of(phase, own, other, first, z_hi)
    z_odd = (space // 4) % 2 == 1
    lane = lane32()
    part = lane // 8
    for slot in range(8):
        n = HALO_PAIRS[slot]
        for f in range(2):
            rows = rows_of(get, odd, even, z_odd, slot, f)
            for index, row in enumerate(rows):
                if slot < 7:
                    at, q = QUAD_AT[slot] + index // 4, index % 4
                    l_halo, r_halo = from_left[at, f], from_right[at, f]
                    if q != 0:
                        l_halo = pltpu.roll(l_halo, 128 - 8 * q, 1)
                    if q != 3:
                        r_halo = pltpu.roll(r_halo, 24 - 8 * q, 1)
                    row = jnp.where(part == 0, l_halo, jnp.where(part == 3, r_halo, row))
                if slot == 0:
                    state[0, f, 8 - 2 * n + index] = row
                else:
                    taus[slot - 1, f, 8 - 2 * n + index] = row

    def emit(k, pair, f, piece):
        x, y, core = pair // 2, k >> 2, k & 1
        out[ring_of(x, y, core), f, pair % 2] = piece

    offset = 0 if phase == 0 else 7
    if phase == 1:
        for i in range(16):
            out[i] = before[i]
    for f in range(2):
        for pair in range(8):
            if phase == 0:
                emit(0, pair, f, get(0, f, pair))

                @pl.when(z_hi == 0)
                def _(f=f, pair=pair):
                    emit(1, pair, f, get(0, f, pair))

            else:

                @pl.when(z_hi == 0)
                def _(f=f, pair=pair):
                    emit(8, pair, f, first[f, pair])

    sub = lax.broadcasted_iota(jnp.int32, (4, 8, 128), 1)
    lanes = lax.broadcasted_iota(jnp.int32, (4, 8, 128), 2)
    is_top, is_bottom = sub == 7, sub == 0
    end_up = is_top & (lanes >= 96)
    end_down = is_bottom & (lanes < 32)

    def z_up(v):
        w = jnp.where(is_bottom, pltpu.roll(v, 96, 2), v)
        return jnp.where(end_up, v, pltpu.roll(w, 7, 1))

    def z_down(v):
        w = jnp.where(is_top, pltpu.roll(v, 32, 2), v)
        return jnp.where(end_down, v, pltpu.roll(w, 1, 1))

    for j in range(1, 8):
        src, dst = (j + 1) % 2, j % 2
        lo, hi = 8 - (7 - j), 24 + (7 - j)
        starts = list(range(lo, hi - 3, 4))
        if starts[-1] + 4 < hi:
            starts.append(hi - 4)
        for r in starts:
            pc, uc = state[src, 0, r : r + 4], state[src, 1, r : r + 4]
            rate = growth(
                pc, uc,
                state[src, 0, r - 1 : r + 3], state[src, 0, r + 1 : r + 5],
                pltpu.roll(pc, 1, 2), pltpu.roll(pc, 127, 2),
                z_down(pc), z_up(pc),
            )
            ulap = (
                (state[src, 1, r - 1 : r + 3] + state[src, 1, r + 1 : r + 5])
                + (pltpu.roll(uc, 1, 2) + pltpu.roll(uc, 127, 2))
                + (z_down(uc) + z_up(uc))
                - 6.0 * uc
            )
            gain = COARSE_RATE * rate
            state[dst, 0, r : r + 4] = pc + gain + taus[j - 1, 0, r : r + 4]
            state[dst, 1, r : r + 4] = (
                uc + (COARSE_RATE * DIFFUSION) * ulap + 0.5 * gain + taus[j - 1, 1, r : r + 4]
            )
        k = 1 + offset + j

        def pack(f, pair, dst=dst):
            low, high = state[dst, f, 8 + 2 * pair], state[dst, f, 9 + 2 * pair]
            return jnp.where(lane < 16, pltpu.roll(low, 120, 1), pltpu.roll(high, 8, 1))

        if phase == 0 and j == 7:
            for f in range(2):
                for pair in range(8):
                    last[f, pair] = pack(f, pair)
        else:

            @pl.when(z_hi == ((k >> 1) & 1))
            def _(k=k, pack=pack):
                for f in range(2):
                    for pair in range(8):
                        emit(k, pair, f, pack(f, pair))


def finish_kernel(start, got, p_out, u_out):
    tm, _ = block_index()

    @pl.when(tm == 0)
    def _():
        p_out[0] = start[0]
        u_out[0] = start[1]

    @pl.when(tm != 0)
    def _():
        for f, out in enumerate((p_out, u_out)):
            for rp in range(2):
                for b in range(4):
                    parts = transpose_lanes([got[8 * b + j, f, rp] for j in range(8)])
                    for g in range(4):
                        for rr in range(2):
                            at = slice(8 * g, 8 * g + 8), slice(128 * b, 128 * b + 128)
                            out[0, 2 * rp + rr, at[0], at[1]] = parts[2 * g + rr]


VMEM = pl.BlockSpec(memory_space=pltpu.VMEM)
SMEM = pl.BlockSpec(memory_space=pltpu.SMEM)


def call(kernel, outs, args, scratch=(), specs=None):
    shapes = [jax.ShapeDtypeStruct(s, jnp.float32) for s in outs]
    return pl.pallas_call(
        kernel,
        out_shape=shapes if len(shapes) > 1 else shapes[0],
        in_specs=specs or [VMEM] * len(args),
        out_specs=[VMEM] * len(shapes) if len(shapes) > 1 else VMEM,
        scratch_shapes=[pltpu.VMEM(s, jnp.float32) for s in scratch],
        compiler_params=pltpu.CompilerParams(vmem_limit_bytes=40 * 1024 * 1024),
    )(*args)


def exchange_rows(payload, axis, pairs):
    odd, even = payload
    got_odd = lax.ppermute(odd, axis, pairs(1))
    got_even = lax.ppermute(even, axis, pairs(0))
    return got_odd, got_even


def local(phase_guess, solute_guess, solute_start, nuclei):
    start = call(
        start_kernel,
        [(2, 4, 32, 512)],
        [nuclei, phase_guess, solute_guess, solute_start],
        specs=[SMEM, VMEM, VMEM, VMEM],
    )
    odd, even = exchange_rows((start, start), "space", space_pairs)
    packed = call(
        relax_kernel,
        [(32, 2, 2, 8, 128)],
        [start, odd, even],
        scratch=[(2, 12, 48, 512), (2, 12, 48, 512), (2, 4, 32, 512)],
    )
    own = lax.all_to_all(packed, AXES, 0, 0, tiled=True, axis_index_groups=PLANE_GROUPS)
    owns = own[:16], own[16:]
    others = [lax.ppermute(part, "tm", ACROSS) for part in owns]

    first, before = [], []
    for phase in range(2):
        known = [owns[phase], others[phase]] + first
        edges = call(
            lambda *refs, phase=phase: edges_kernel(phase, *refs), [(16, 2, 8, 128)] * 2, known
        )
        known += exchange_rows(edges, AXES, row_pairs)
        right, left = call(
            lambda *refs, phase=phase: lanes_kernel(phase, *refs), [(44, 2, 8, 128)] * 2, known
        )
        known += [lax.ppermute(right, AXES, RIGHT), lax.ppermute(left, AXES, LEFT)]
        outs = [(32, 2, 2, 8, 128)] if phase else [(16, 2, 2, 8, 128), (2, 8, 8, 128)]
        got = call(
            lambda *refs, phase=phase: chain_kernel(phase, *refs),
            outs,
            known + before,
            scratch=[(2, 2, 32, 8, 128), (7, 2, 32, 8, 128)],
        )
        if phase == 0:
            before, first = [got[0]], [got[1]]
    back = lax.all_to_all(got, AXES, 0, 0, tiled=True, axis_index_groups=PLANE_GROUPS)
    return call(finish_kernel, [(1, 4, 32, 512)] * 2, [start, back])


def solution(mesh):
    return jax.shard_map(
        lambda *args: tuple(local(*args)),
        mesh=mesh,
        in_specs=(
            P("tm", "space", None, None),
            P("tm", "space", None, None),
            P("space", None, None),
            P(),
        ),
        out_specs=(P("tm", "space", None, None), P("tm", "space", None, None)),
        check_vma=False,
    )
```

```python
import jax
import jax.numpy as jnp
from jax import lax
from jax.experimental import pallas as pl
from jax.experimental.pallas import tpu as pltpu
from jax.sharding import PartitionSpec as P

M = 4
FINE_RATE = 0.025
COARSE_RATE = M * FINE_RATE
DIFFUSION = 1.5
WIDTH_SQ = 18.0
AXES = ("tm", "space")


def device(x, y, z_lo, z_hi, core):
    return (y * 4 + z_hi * 2 + core) * 32 + z_lo * 4 + x


def ring_of(x, y, core):
    return 2 * (y * 4 + (3 - x if y & 1 else x)) + core


def place(ring):
    q, core = ring >> 1, ring & 1
    y, x = q >> 2, q & 3
    return (3 - x if y & 1 else x), y, core


PLANES = [(z_lo, z_hi) for z_hi in range(2) for z_lo in range(8)]


def on_ring(ring, plane):
    x, y, core = place(ring % 32)
    return device(x, y, plane[0], plane[1], core)


RING = [ring_of(n % 4, n // 8, (n // 4) % 2) for n in range(32)]
MEMBER = [RING.index(i) for i in range(32)]
PLANE_GROUPS = [[on_ring(i, plane) for i in RING] for plane in PLANES]
RIGHT = [(on_ring(i, plane), on_ring(i + 1, plane)) for plane in PLANES for i in range(32)]
LEFT = [(b, a) for a, b in RIGHT]
ACROSS = [(i, i ^ 2) for i in range(16)]


def row_pairs(parity):
    pairs = []
    for z in range(parity, 16, 2):
        for i in range(32):
            a, b = on_ring(i, (z % 8, z // 8)), on_ring(i, ((z + 1) % 8, (z + 1) // 8 % 2))
            pairs += [(a, b), (b, a)]
    return pairs


def space_pairs(parity):
    pairs = []
    for s in range(parity, 32, 2):
        pairs += [(s, (s + 1) % 32), ((s + 1) % 32, s)]
    return pairs


def growth(pc, uc, pxm, pxp, pym, pyp, pzm, pzp):
    dx, dy, dz = pxp - pxm, pyp - pym, pzp - pzm
    dx, dy, dz = dx * dx, dy * dy, dz * dz
    floor = jnp.maximum(dx + dy + dz, 0.04)
    quartic = (dx * dx + dy * dy + dz * dz) / (floor * floor)
    aniso = 0.85 + 0.2 * quartic
    lap = ((pxp + pxm) + (pyp + pym)) + (pzp + pzm) - 6.0 * pc
    wet = 1.0 - pc * pc
    return aniso * aniso * lap + wet * (pc - 2.0 * uc * wet)


def block_index():
    return lax.axis_index("tm"), lax.axis_index("space")


def start_kernel(nuclei, p_in, u_in, u_start, out, cells, sems):
    tm, space = block_index()
    whole = (tm == 0) | (tm == 15)

    @pl.when(~whole)
    def _():
        p_copy = pltpu.make_async_copy(p_in.at[0], out.at[0], sems.at[0])
        u_copy = pltpu.make_async_copy(u_in.at[0], out.at[1], sems.at[1])
        p_copy.start()
        u_copy.start()
        p_copy.wait()
        u_copy.wait()

    @pl.when(whole)
    def _():
        u_copy = pltpu.make_async_copy(u_start, out.at[1], sems.at[1])
        n_copy = pltpu.make_async_copy(nuclei, cells, sems.at[0])
        u_copy.start()
        n_copy.start()
        n_copy.wait()
        zs = lax.broadcasted_iota(jnp.int32, (8, 512), 0)
        ys = lax.broadcasted_iota(jnp.int32, (8, 512), 1)
        for g in range(4):
            sides = []
            for n in range(8):
                dy = jnp.abs(ys - cells[2, n])
                dy = jnp.minimum(dy, 512 - dy)
                dz = zs + 8 * g - cells[1, n]
                sides.append(dy * dy + dz * dz)
            for r in range(4):
                best = None
                for n in range(8):
                    dx = jnp.abs(space * 4 + r - cells[0, n])
                    dx = jnp.minimum(dx, 128 - dx)
                    here = sides[n] + dx * dx
                    best = here if best is None else jnp.minimum(best, here)
                b = jnp.exp(-best.astype(jnp.float32) / WIDTH_SQ)
                out[0, r, 8 * g : 8 * g + 8, :] = 2.0 * b - 1.0
        u_copy.wait()


def transpose_lanes(parts):
    slot = lax.broadcasted_iota(jnp.int32, (8, 128), 1) // 16
    parts = list(parts)
    for d in (4, 2, 1):
        low = (slot & d) == 0
        for a in range(8):
            if not a & d:
                top, bottom = parts[a], parts[a + d]
                parts[a] = jnp.where(low, top, pltpu.roll(bottom, 16 * d, 1))
                parts[a + d] = jnp.where(low, pltpu.roll(top, 128 - 16 * d, 1), bottom)
    return parts


def relax_kernel(start, odd, even, out, one, two, coarse):
    tm, space = block_index()
    keep = jnp.where((tm == 0) | (tm == 15), 0.0, 1.0)

    def put(buf, f, row, g, value):
        buf[f, row, 8 + 8 * g : 16 + 8 * g, :] = value
        if g == 0:
            buf[f, row, 7:8, :] = value[0:1]
        if g == 3:
            buf[f, row, 40:41, :] = value[7:8]

    def fill(before, after):
        for f in range(2):
            for part, src in enumerate((before, start, after)):
                for r in range(4):
                    for g in range(4):
                        put(one, f, 4 * part + r, g, src[f, r, 8 * g : 8 * g + 8, :])

    @pl.when(space % 2 == 0)
    def _():
        fill(odd, even)

    @pl.when(space % 2 == 1)
    def _():
        fill(even, odd)

    def one_row(src, dst, row, first):
        for g in range(4):
            at = slice(8 + 8 * g, 16 + 8 * g)
            up = slice(9 + 8 * g, 17 + 8 * g)
            down = slice(7 + 8 * g, 15 + 8 * g)
            pc, uc = src[0, row, at, :], src[1, row, at, :]
            rate = growth(
                pc, uc,
                src[0, row - 1, at, :], src[0, row + 1, at, :],
                pltpu.roll(pc, 1, 1), pltpu.roll(pc, 511, 1),
                src[0, row, down, :], src[0, row, up, :],
            )
            ulap = (
                (src[1, row - 1, at, :] + src[1, row + 1, at, :])
                + (pltpu.roll(uc, 1, 1) + pltpu.roll(uc, 511, 1))
                + (src[1, row, down, :] + src[1, row, up, :])
                - 6.0 * uc
            )
            gain = FINE_RATE * rate
            put(dst, 0, row, g, pc + gain)
            put(dst, 1, row, g, uc + (FINE_RATE * DIFFUSION) * ulap + 0.5 * gain)
            if first:
                gain = COARSE_RATE * rate
                coarse[0, row - 4, 8 * g : 8 * g + 8, :] = pc + gain
                coarse[1, row - 4, 8 * g : 8 * g + 8, :] = (
                    uc + (COARSE_RATE * DIFFUSION) * ulap + 0.5 * gain
                )

    def sweep(src, dst, lo, hi, first=False):
        @pl.loop(lo, hi)
        def _(row):
            one_row(src, dst, row, first)

    sweep(one, two, 1, 4)
    sweep(one, two, 4, 8, True)
    sweep(one, two, 8, 11)
    sweep(two, one, 2, 10)
    sweep(one, two, 3, 9)
    sweep(two, one, 4, 8)

    for f in range(2):
        for rp in range(2):
            for b in range(4):
                parts = []
                for g in range(4):
                    for rr in range(2):
                        r = 2 * rp + rr
                        lanes = slice(128 * b, 128 * b + 128)
                        fine = one[f, 4 + r, 8 + 8 * g : 16 + 8 * g, lanes]
                        parts.append(fine - keep * coarse[f, r, 8 * g : 8 * g + 8, lanes])
                for j, part in enumerate(transpose_lanes(parts)):
                    out[MEMBER[8 * b + j], f, rp] = part


STEPS = (6, 8)


class Phase:
    def __init__(self, index):
        self.index = index
        self.steps = STEPS[index]
        self.base = 1 + index * STEPS[0]
        self.halo = [self.steps - j for j in range(self.steps + 1)]
        self.halo_at = [sum(self.halo[:j]) for j in range(self.steps + 2)]


PHASES = Phase(0), Phase(1)


def half_of(k):
    return (k >> 1) & 1


def local_block(k):
    return 2 * (k >> 2) + (k & 1)


def lane32():
    return lax.broadcasted_iota(jnp.int32, (8, 128), 1) % 32


def piece_of(phase, own, other, first, z_hi):
    def get(slot, f, pair):
        x, rp = pair // 2, pair % 2
        if slot == 0 and phase.index:
            return first[f, pair]
        if slot == 0:
            return jnp.where(z_hi == 0, own[x, f, rp], own[28 + x, f, rp])
        k = phase.base + slot - 1
        m = local_block(k)
        sent = m - (4 * phase.index + (1 - phase.index) - half_of(k) * 1)
        return jnp.where(
            half_of(k) == z_hi, own[4 * m + x, f, rp], other[4 * sent + x, f, rp]
        )

    return get


def sent_from(phase, z_hi):
    return 4 * (4 * phase.index + (1 - phase.index) - z_hi)


def split(phase, refs, count):
    if phase.index == 0:
        return refs[0], refs[1], None, *refs[2 : 2 + count]
    return refs[0], refs[1], refs[2], *refs[3 : 3 + count]


def cut_kernel(own, near, middle, far, once, *blank):
    tm, _ = block_index()
    z_hi = (tm // 2) % 2
    at = 4 * (1 - z_hi)
    for out in (near, middle, far):
        out[...] = own[pl.ds(at, out.shape[0])]
        at = at + out.shape[0]
    once[0] = 1


def lanes_kernel(phase, *refs):
    own, other, first, right, left = split(phase, refs, 2)
    tm, _ = block_index()
    get = piece_of(phase, own, other, first, (tm // 2) % 2)
    part = lane32() // 8
    for slot in range(phase.steps):
        for f in range(2):
            for quad in range(4):
                r_edge = l_edge = None
                for q in range(4):
                    if q % 2 == 0:
                        piece = get(slot, f, 2 * quad + q // 2)
                    at = 16 * (q % 2)
                    r_part = pltpu.roll(piece, (8 * q - at - 8) % 128, 1)
                    l_part = pltpu.roll(piece, (8 * q - at) % 128, 1) if 8 * q != at else piece
                    if q == 0:
                        r_edge, l_edge = r_part, l_part
                    else:
                        r_edge = jnp.where(part == q, r_part, r_edge)
                        l_edge = jnp.where(part == q, l_part, l_edge)
                right[4 * slot + quad, f] = r_edge
                left[4 * slot + quad, f] = l_edge


def row_of(phase, get, from_left, from_right):
    part = lane32() // 8

    def row(slot, f, r):
        value = pltpu.roll(get(slot, f, r // 2), 120 if r % 2 else 8, 1)
        if slot == phase.steps:
            return value
        quad, q = 4 * slot + r // 4, r % 4
        l_halo, r_halo = from_left[quad, f], from_right[quad, f]
        if q != 0:
            l_halo = pltpu.roll(l_halo, 128 - 8 * q, 1)
        if q != 3:
            r_halo = pltpu.roll(r_halo, 24 - 8 * q, 1)
        return jnp.where(part == 0, l_halo, jnp.where(part == 3, r_halo, value))

    return row


def edges_kernel(phase, *refs):
    own, other, first, from_left, from_right, odd, even = split(phase, refs, 4)
    tm, space = block_index()
    get = piece_of(phase, own, other, first, (tm // 2) % 2)
    row = row_of(phase, get, from_left, from_right)
    z_odd = (space // 4) % 2 == 1
    for slot in range(phase.steps):
        n = phase.halo[slot]
        for f in range(2):
            for m in range(n):
                top, bottom = row(slot, f, m), row(slot, f, 16 - n + m)
                odd[phase.halo_at[slot] + m, f] = jnp.where(z_odd, bottom, top)
                even[phase.halo_at[slot] + m, f] = jnp.where(z_odd, top, bottom)


def chain_kernel(phase, *refs):
    if phase.index == 0:
        own, other, first, from_left, from_right, odd, even, out, last, state, taus = split(
            phase, refs, 8
        )
    else:
        own, other, first, from_left, from_right, odd, even, before, out, state, taus = split(
            phase, refs, 8
        )
    tm, space = block_index()
    z_hi = (tm // 2) % 2
    get = piece_of(phase, own, other, first, z_hi)
    row = row_of(phase, get, from_left, from_right)
    z_odd = (space // 4) % 2 == 1
    lane = lane32()
    for slot in range(phase.steps + 1):
        n, at = phase.halo[slot], phase.halo_at[slot]
        for f in range(2):
            put = state.at[0, f] if slot == 0 else taus.at[slot - 1, f]
            for m in range(n):
                put[8 - n + m] = jnp.where(z_odd, even[at + m, f], odd[at + m, f])
                put[24 + m] = jnp.where(z_odd, odd[at + m, f], even[at + m, f])
            for r in range(16):
                put[8 + r] = row(slot, f, r)

    def emit(k, pair, f, piece):
        out[4 * local_block(k) + pair // 2, f, pair % 2] = piece

    if phase.index:
        for i in range(16):
            out[i] = before[i]

    def given():
        for f in range(2):
            for pair in range(8):
                emit(phase.base, pair, f, get(0, f, pair))
                if phase.index == 0:
                    emit(0, pair, f, get(0, f, pair))

    pl.when(z_hi == half_of(phase.base))(given)

    sub = lax.broadcasted_iota(jnp.int32, (4, 8, 128), 1)
    lanes = lax.broadcasted_iota(jnp.int32, (4, 8, 128), 2)
    is_top, is_bottom = sub == 7, sub == 0
    end_up = is_top & (lanes >= 96)
    end_down = is_bottom & (lanes < 32)

    def z_up(v):
        w = jnp.where(is_bottom, pltpu.roll(v, 96, 2), v)
        return jnp.where(end_up, v, pltpu.roll(w, 7, 1))

    def z_down(v):
        w = jnp.where(is_top, pltpu.roll(v, 32, 2), v)
        return jnp.where(end_down, v, pltpu.roll(w, 1, 1))

    for j in range(1, phase.steps + 1):
        src, dst = (j + 1) % 2, j % 2
        lo, hi = 8 - (phase.steps - j), 24 + (phase.steps - j)
        starts = list(range(lo, hi - 3, 4))
        if starts[-1] + 4 < hi:
            starts.append(hi - 4)
        for r in starts:
            pc, uc = state[src, 0, r : r + 4], state[src, 1, r : r + 4]
            rate = growth(
                pc, uc,
                state[src, 0, r - 1 : r + 3], state[src, 0, r + 1 : r + 5],
                pltpu.roll(pc, 1, 2), pltpu.roll(pc, 127, 2),
                z_down(pc), z_up(pc),
            )
            ulap = (
                (state[src, 1, r - 1 : r + 3] + state[src, 1, r + 1 : r + 5])
                + (pltpu.roll(uc, 1, 2) + pltpu.roll(uc, 127, 2))
                + (z_down(uc) + z_up(uc))
                - 6.0 * uc
            )
            gain = COARSE_RATE * rate
            state[dst, 0, r : r + 4] = pc + gain + taus[j - 1, 0, r : r + 4]
            state[dst, 1, r : r + 4] = (
                uc + (COARSE_RATE * DIFFUSION) * ulap + 0.5 * gain + taus[j - 1, 1, r : r + 4]
            )
        k = phase.base + j

        def pack(f, pair, dst=dst):
            low, high = state[dst, f, 8 + 2 * pair], state[dst, f, 9 + 2 * pair]
            return jnp.where(lane < 16, pltpu.roll(low, 120, 1), pltpu.roll(high, 8, 1))

        if phase.index == 0 and j == phase.steps:
            for f in range(2):
                for pair in range(8):
                    last[f, pair] = pack(f, pair)
        else:

            @pl.when(z_hi == half_of(k))
            def _(k=k, pack=pack):
                for f in range(2):
                    for pair in range(8):
                        emit(k, pair, f, pack(f, pair))


def finish_kernel(start, got, p_out, u_out):
    tm, _ = block_index()

    @pl.when(tm == 0)
    def _():
        p_out[0] = start[0]
        u_out[0] = start[1]

    @pl.when(tm != 0)
    def _():
        for f, out in enumerate((p_out, u_out)):
            for rp in range(2):
                for b in range(4):
                    parts = transpose_lanes([got[MEMBER[8 * b + j], f, rp] for j in range(8)])
                    for g in range(4):
                        for rr in range(2):
                            at = slice(8 * g, 8 * g + 8), slice(128 * b, 128 * b + 128)
                            out[0, 2 * rp + rr, at[0], at[1]] = parts[2 * g + rr]


VMEM = pl.BlockSpec(memory_space=pltpu.VMEM)
ANY = pl.BlockSpec(memory_space=pl.ANY)


def call(kernel, outs, args, scratch=(), specs=None, grant=40):
    shapes = [jax.ShapeDtypeStruct(s, jnp.float32) for s in outs]
    return pl.pallas_call(
        kernel,
        out_shape=shapes if len(shapes) > 1 else shapes[0],
        in_specs=specs or [VMEM] * len(args),
        out_specs=[VMEM] * len(shapes) if len(shapes) > 1 else VMEM,
        scratch_shapes=[pltpu.VMEM(s, jnp.float32) if isinstance(s, tuple) else s for s in scratch],
        cost_estimate=pl.CostEstimate(flops=8, bytes_accessed=8, transcendentals=0),
        compiler_params=pltpu.CompilerParams(vmem_limit_bytes=grant * 1024 * 1024),
    )(*args)


def exchange_rows(payload, axis, pairs):
    odd, even = payload
    got_odd = lax.ppermute(odd, axis, pairs(1))
    got_even = lax.ppermute(even, axis, pairs(0))
    return got_odd, got_even


def local(phase_guess, solute_guess, solute_start, nuclei):
    start = call(
        start_kernel,
        [(2, 4, 32, 512)],
        [nuclei.T, phase_guess, solute_guess, solute_start],
        scratch=[pltpu.SMEM((3, 8), jnp.int32), pltpu.SemaphoreType.DMA((2,))],
        specs=[ANY] * 4,
        grant=60,
    )
    odd, even = exchange_rows((start, start), "space", space_pairs)
    packed = call(
        relax_kernel,
        [(32, 2, 2, 8, 128)],
        [start, odd, even],
        scratch=[(2, 12, 48, 512), (2, 12, 48, 512), (2, 4, 32, 512)],
    )
    own = lax.all_to_all(packed, AXES, 0, 0, tiled=True, axis_index_groups=PLANE_GROUPS)
    blank = [(16, 2, 2, 8, 128), (2, 8, 8, 128)]
    shapes = [(4 * blocks, 2, 2, 8, 128) for blocks in (2, 1, 4)]
    near, middle, far, once, *blank = pl.pallas_call(
        cut_kernel,
        out_shape=[jax.ShapeDtypeStruct(s, jnp.float32) for s in shapes]
        + [jax.ShapeDtypeStruct((1,), jnp.int32)]
        + [jax.ShapeDtypeStruct(s, jnp.float32) for s in blank],
        in_specs=[VMEM],
        out_specs=[VMEM, VMEM, VMEM, pl.BlockSpec(memory_space=pltpu.SMEM), ANY, ANY],
        compiler_params=pltpu.CompilerParams(vmem_limit_bytes=40 * 1024 * 1024),
    )(own)
    near = lax.ppermute(near, "tm", ACROSS)
    middle = lax.ppermute(middle, "tm", ACROSS)

    def lanes(phase, known):
        right, left = call(
            lambda *refs: lanes_kernel(phase, *refs), [(4 * phase.steps, 2, 8, 128)] * 2, known
        )
        return [lax.ppermute(right, AXES, RIGHT), lax.ppermute(left, AXES, LEFT)]

    def advance(phase, known, before=(), after=()):
        edges = call(
            lambda *refs: edges_kernel(phase, *refs[len(after) :]),
            [(phase.halo_at[-1], 2, 8, 128)] * 2,
            [*after, *known],
            specs=[ANY] * len(after) + [VMEM] * len(known),
        )
        return call(
            lambda *refs: chain_kernel(phase, *refs),
            [(32, 2, 2, 8, 128)] if phase.index else [(16, 2, 2, 8, 128), (2, 8, 8, 128)],
            [*known, *exchange_rows(edges, AXES, row_pairs), *before],
            scratch=[(2, 2, 32, 8, 128), (phase.steps, 2, 32, 8, 128)],
        )

    known = [own, jnp.concatenate([near, middle])]
    far, _ = lax.optimization_barrier((far, near))
    crossed = lax.ppermute(far, "tm", ACROSS)
    known += lanes(PHASES[0], known)
    before, first = lax.fori_loop(
        0, once[0], lambda i, state: tuple(advance(PHASES[0], known, (), state[1:])), tuple(blank)
    )
    known = [own, crossed, first]
    known += lanes(PHASES[1], known)
    got = advance(PHASES[1], known, [before])
    back = lax.all_to_all(got, AXES, 0, 0, tiled=True, axis_index_groups=PLANE_GROUPS)
    return call(finish_kernel, [(1, 4, 32, 512)] * 2, [start, back])


def solution(mesh):
    return jax.shard_map(
        lambda *args: tuple(local(*args)),
        mesh=mesh,
        in_specs=(
            P("tm", "space", None, None),
            P("tm", "space", None, None),
            P("space", None, None),
            P(),
        ),
        out_specs=(P("tm", "space", None, None), P("tm", "space", None, None)),
        check_vma=False,
    )
```

```python
import jax
import jax.numpy as jnp
from jax import lax
from jax.experimental import pallas as pl
from jax.experimental.pallas import tpu as pltpu
from jax.sharding import PartitionSpec as P

M = 4
FINE_RATE = 0.025
COARSE_RATE = M * FINE_RATE
DIFFUSION = 1.5
WIDTH_SQ = 18.0
AXES = ("tm", "space")


def device(x, y, z_lo, z_hi, core):
    return (y * 4 + z_hi * 2 + core) * 32 + z_lo * 4 + x


def ring_of(x, y, core):
    return 2 * (y * 4 + (3 - x if y & 1 else x)) + core


def place(ring):
    q, core = ring >> 1, ring & 1
    y, x = q >> 2, q & 3
    return (3 - x if y & 1 else x), y, core


PLANES = [(z_lo, z_hi) for z_hi in range(2) for z_lo in range(8)]


def on_ring(ring, plane):
    x, y, core = place(ring % 32)
    return device(x, y, plane[0], plane[1], core)


RING = [ring_of(n % 4, n // 8, (n // 4) % 2) for n in range(32)]
MEMBER = [RING.index(i) for i in range(32)]
PLANE_GROUPS = [[on_ring(i, plane) for i in RING] for plane in PLANES]
RIGHT = [(on_ring(i, plane), on_ring(i + 1, plane)) for plane in PLANES for i in range(32)]
LEFT = [(b, a) for a, b in RIGHT]
ACROSS = [(i, i ^ 2) for i in range(16)]


def row_pairs(parity):
    pairs = []
    for z in range(parity, 16, 2):
        for i in range(32):
            a, b = on_ring(i, (z % 8, z // 8)), on_ring(i, ((z + 1) % 8, (z + 1) // 8 % 2))
            pairs += [(a, b), (b, a)]
    return pairs


def space_pairs(parity):
    pairs = []
    for s in range(parity, 32, 2):
        pairs += [(s, (s + 1) % 32), ((s + 1) % 32, s)]
    return pairs


def growth(pc, uc, pxm, pxp, pym, pyp, pzm, pzp):
    dx, dy, dz = pxp - pxm, pyp - pym, pzp - pzm
    dx, dy, dz = dx * dx, dy * dy, dz * dz
    floor = jnp.maximum(dx + dy + dz, 0.04)
    quartic = (dx * dx + dy * dy + dz * dz) / (floor * floor)
    aniso = 0.85 + 0.2 * quartic
    lap = ((pxp + pxm) + (pyp + pym)) + (pzp + pzm) - 6.0 * pc
    wet = 1.0 - pc * pc
    return aniso * aniso * lap + wet * (pc - 2.0 * uc * wet)


def block_index():
    return lax.axis_index("tm"), lax.axis_index("space")


def start_kernel(nuclei, p_in, u_in, u_start, out, cells, made, sems):
    tm, space = block_index()
    whole = (tm == 0) | (tm == 15)

    def move(f, r, source=None):
        rows = pl.ds(2 * r, 2)
        if source is None:
            return pltpu.make_async_copy(made.at[f, rows], out.at[f, rows], sems.at[2 * f + r])
        return pltpu.make_async_copy(source.at[rows], made.at[f, rows], sems.at[4 + 2 * f + r])

    def through(fields):
        for f, source in fields:
            for r in range(2):
                move(f, r, source).start()
        for f, source in fields:
            for r in range(2):
                move(f, r, source).wait()
                move(f, r).start()

    @pl.when(~whole)
    def _():
        through([(0, p_in.at[0]), (1, u_in.at[0])])

    @pl.when(whole)
    def _():
        n_copy = pltpu.make_async_copy(nuclei, cells, sems.at[8])
        n_copy.start()
        through([(1, u_start)])
        n_copy.wait()
        zs = lax.broadcasted_iota(jnp.int32, (8, 512), 0)
        ys = lax.broadcasted_iota(jnp.int32, (8, 512), 1)
        for g in range(4):
            sides = []
            for n in range(8):
                dy = jnp.abs(ys - cells[2, n])
                dy = jnp.minimum(dy, 512 - dy)
                dz = zs + 8 * g - cells[1, n]
                sides.append(dy * dy + dz * dz)
            for r in range(4):
                best = None
                for n in range(8):
                    dx = jnp.abs(space * 4 + r - cells[0, n])
                    dx = jnp.minimum(dx, 128 - dx)
                    here = sides[n] + dx * dx
                    best = here if best is None else jnp.minimum(best, here)
                b = jnp.exp(-best.astype(jnp.float32) / WIDTH_SQ)
                made[0, r, 8 * g : 8 * g + 8, :] = 2.0 * b - 1.0
        for r in range(2):
            move(0, r).start()

    for f in range(2):
        for r in range(2):
            move(f, r).wait()


def transpose_lanes(parts):
    slot = lax.broadcasted_iota(jnp.int32, (8, 128), 1) // 16
    parts = [pltpu.roll(part, 16 * a, 1) if a else part for a, part in enumerate(parts)]
    for d in (1, 2, 4):
        move = (slot & d) != 0
        parts = [jnp.where(move, parts[(i + d) % 8], parts[i]) for i in range(8)]
    return [
        pltpu.roll(parts[-j % 8], 128 - 16 * j, 1) if j else parts[0] for j in range(8)
    ]


def relax_kernel(start, odd, even, out, one, two, coarse):
    tm, space = block_index()
    keep = jnp.where((tm == 0) | (tm == 15), 0.0, 1.0)

    def put(buf, f, row, g, value):
        buf[f, row, 8 + 8 * g : 16 + 8 * g, :] = value
        if g == 0:
            buf[f, row, 7:8, :] = value[0:1]
        if g == 3:
            buf[f, row, 40:41, :] = value[7:8]

    def fill(before, after):
        for f in range(2):
            for part, src in enumerate((before, start, after)):
                for r in range(4):
                    for g in range(4):
                        put(one, f, 4 * part + r, g, src[f, r, 8 * g : 8 * g + 8, :])

    @pl.when(space % 2 == 0)
    def _():
        fill(odd, even)

    @pl.when(space % 2 == 1)
    def _():
        fill(even, odd)

    def one_row(src, dst, row, first):
        for g in range(4):
            at = slice(8 + 8 * g, 16 + 8 * g)
            up = slice(9 + 8 * g, 17 + 8 * g)
            down = slice(7 + 8 * g, 15 + 8 * g)
            pc, uc = src[0, row, at, :], src[1, row, at, :]
            rate = growth(
                pc, uc,
                src[0, row - 1, at, :], src[0, row + 1, at, :],
                pltpu.roll(pc, 1, 1), pltpu.roll(pc, 511, 1),
                src[0, row, down, :], src[0, row, up, :],
            )
            ulap = (
                (src[1, row - 1, at, :] + src[1, row + 1, at, :])
                + (pltpu.roll(uc, 1, 1) + pltpu.roll(uc, 511, 1))
                + (src[1, row, down, :] + src[1, row, up, :])
                - 6.0 * uc
            )
            gain = FINE_RATE * rate
            put(dst, 0, row, g, pc + gain)
            put(dst, 1, row, g, uc + (FINE_RATE * DIFFUSION) * ulap + 0.5 * gain)
            if first:
                gain = COARSE_RATE * rate
                coarse[0, row - 4, 8 * g : 8 * g + 8, :] = pc + gain
                coarse[1, row - 4, 8 * g : 8 * g + 8, :] = (
                    uc + (COARSE_RATE * DIFFUSION) * ulap + 0.5 * gain
                )

    def sweep(src, dst, lo, hi, first=False):
        @pl.loop(lo, hi)
        def _(row):
            one_row(src, dst, row, first)

    sweep(one, two, 1, 4)
    sweep(one, two, 4, 8, True)
    sweep(one, two, 8, 11)
    sweep(two, one, 2, 10)
    sweep(one, two, 3, 9)
    sweep(two, one, 4, 8)

    for f in range(2):
        for rp in range(2):
            for b in range(4):
                parts = []
                for g in range(4):
                    for rr in range(2):
                        r = 2 * rp + rr
                        lanes = slice(128 * b, 128 * b + 128)
                        fine = one[f, 4 + r, 8 + 8 * g : 16 + 8 * g, lanes]
                        parts.append(fine - keep * coarse[f, r, 8 * g : 8 * g + 8, lanes])
                for j, part in enumerate(transpose_lanes(parts)):
                    out[MEMBER[8 * b + j], f, rp] = part


STEPS = (6, 8)


class Phase:
    def __init__(self, index):
        self.index = index
        self.steps = STEPS[index]
        self.base = 1 + index * STEPS[0]
        self.halo = [self.steps - j for j in range(self.steps + 1)]
        self.halo_at = [sum(self.halo[:j]) for j in range(self.steps + 2)]


PHASES = Phase(0), Phase(1)


def half_of(k):
    return (k >> 1) & 1


def local_block(k):
    return 2 * (k >> 2) + (k & 1)


def lane32():
    return lax.broadcasted_iota(jnp.int32, (8, 128), 1) % 32


def piece_of(phase, own, other, first, z_hi):
    def get(slot, f, pair):
        x, rp = pair // 2, pair % 2
        if slot == 0 and phase.index:
            return first[f, pair]
        if slot == 0:
            return jnp.where(z_hi == 0, own[x, f, rp], own[28 + x, f, rp])
        k = phase.base + slot - 1
        m = local_block(k)
        sent = m - (4 * phase.index + (1 - phase.index) - half_of(k) * 1)
        return jnp.where(
            half_of(k) == z_hi, own[4 * m + x, f, rp], other[4 * sent + x, f, rp]
        )

    return get


def sent_from(phase, z_hi):
    return 4 * (4 * phase.index + (1 - phase.index) - z_hi)


def split(phase, refs, count):
    if phase.index == 0:
        return refs[0], refs[1], None, *refs[2 : 2 + count]
    return refs[0], refs[1], refs[2], *refs[3 : 3 + count]


def cut_kernel(own, near, middle, far, once, *blank):
    tm, _ = block_index()
    z_hi = (tm // 2) % 2
    at = 4 * (1 - z_hi)
    for out in (near, middle, far):
        out[...] = own[pl.ds(at, out.shape[0])]
        at = at + out.shape[0]
    once[0] = 1


def lanes_kernel(phase, *refs):
    own, other, first, right, left = split(phase, refs, 2)
    tm, _ = block_index()
    get = piece_of(phase, own, other, first, (tm // 2) % 2)
    part = lane32() // 8
    for slot in range(phase.steps):
        for f in range(2):
            for quad in range(4):
                r_edge = l_edge = None
                for q in range(4):
                    if q % 2 == 0:
                        piece = get(slot, f, 2 * quad + q // 2)
                    at = 16 * (q % 2)
                    r_part = pltpu.roll(piece, (8 * q - at - 8) % 128, 1)
                    l_part = pltpu.roll(piece, (8 * q - at + 24) % 128, 1)
                    if q == 0:
                        r_edge, l_edge = r_part, l_part
                    else:
                        r_edge = jnp.where(part == q, r_part, r_edge)
                        l_edge = jnp.where(part == (q + 3) % 4, l_part, l_edge)
                right[4 * slot + quad, f] = r_edge
                left[4 * slot + quad, f] = l_edge


def row_of(phase, get, from_left, from_right):
    part = lane32() // 8

    def row(slot, f, r):
        value = pltpu.roll(get(slot, f, r // 2), 120 if r % 2 else 8, 1)
        if slot == phase.steps:
            return value
        quad, q = 4 * slot + r // 4, r % 4
        halo = jnp.where(part == q, from_left[quad, f], from_right[quad, f])
        if q != 0:
            halo = pltpu.roll(halo, 128 - 8 * q, 1)
        return jnp.where((part == 0) | (part == 3), halo, value)

    return row


def edges_kernel(phase, *refs):
    own, other, first, from_left, from_right, odd, even = split(phase, refs, 4)
    tm, space = block_index()
    get = piece_of(phase, own, other, first, (tm // 2) % 2)
    row = row_of(phase, get, from_left, from_right)
    z_odd = (space // 4) % 2 == 1
    for slot in range(phase.steps):
        n = phase.halo[slot]
        for f in range(2):
            for m in range(n):
                top, bottom = row(slot, f, m), row(slot, f, 16 - n + m)
                odd[phase.halo_at[slot] + m, f] = jnp.where(z_odd, bottom, top)
                even[phase.halo_at[slot] + m, f] = jnp.where(z_odd, top, bottom)


def chain_kernel(phase, *refs):
    if phase.index == 0:
        own, other, first, from_left, from_right, odd, even, out, last, state, taus = split(
            phase, refs, 8
        )
    else:
        own, other, first, from_left, from_right, odd, even, before, out, state, taus = split(
            phase, refs, 8
        )
    tm, space = block_index()
    z_hi = (tm // 2) % 2
    get = piece_of(phase, own, other, first, z_hi)
    row = row_of(phase, get, from_left, from_right)
    z_odd = (space // 4) % 2 == 1
    lane = lane32()
    for slot in range(phase.steps + 1):
        n, at = phase.halo[slot], phase.halo_at[slot]
        for f in range(2):
            put = state.at[0, f] if slot == 0 else taus.at[slot - 1, f]
            for m in range(n):
                put[8 - n + m] = jnp.where(z_odd, even[at + m, f], odd[at + m, f])
                put[24 + m] = jnp.where(z_odd, odd[at + m, f], even[at + m, f])
            for r in range(16):
                put[8 + r] = row(slot, f, r)

    def emit(k, pair, f, piece):
        out[4 * local_block(k) + pair // 2, f, pair % 2] = piece

    if phase.index:
        for i in range(16):
            out[i] = before[i]

    def given():
        for f in range(2):
            for pair in range(8):
                emit(phase.base, pair, f, get(0, f, pair))
                if phase.index == 0:
                    emit(0, pair, f, get(0, f, pair))

    pl.when(z_hi == half_of(phase.base))(given)

    sub = lax.broadcasted_iota(jnp.int32, (4, 8, 128), 1)
    lanes = lax.broadcasted_iota(jnp.int32, (4, 8, 128), 2)
    is_top, is_bottom = sub == 7, sub == 0
    end_up = is_top & (lanes >= 96)
    end_down = is_bottom & (lanes < 32)

    def z_up(v):
        w = jnp.where(is_bottom, pltpu.roll(v, 96, 2), v)
        return jnp.where(end_up, v, pltpu.roll(w, 7, 1))

    def z_down(v):
        w = jnp.where(is_top, pltpu.roll(v, 32, 2), v)
        return jnp.where(end_down, v, pltpu.roll(w, 1, 1))

    for j in range(1, phase.steps + 1):
        src, dst = (j + 1) % 2, j % 2
        lo, hi = 8 - (phase.steps - j), 24 + (phase.steps - j)
        starts = list(range(lo, hi - 3, 4))
        if starts[-1] + 4 < hi:
            starts.append(hi - 4)
        for r in starts:
            pc, uc = state[src, 0, r : r + 4], state[src, 1, r : r + 4]
            rate = growth(
                pc, uc,
                state[src, 0, r - 1 : r + 3], state[src, 0, r + 1 : r + 5],
                pltpu.roll(pc, 1, 2), pltpu.roll(pc, 127, 2),
                z_down(pc), z_up(pc),
            )
            ulap = (
                (state[src, 1, r - 1 : r + 3] + state[src, 1, r + 1 : r + 5])
                + (pltpu.roll(uc, 1, 2) + pltpu.roll(uc, 127, 2))
                + (z_down(uc) + z_up(uc))
                - 6.0 * uc
            )
            gain = COARSE_RATE * rate
            state[dst, 0, r : r + 4] = pc + gain + taus[j - 1, 0, r : r + 4]
            state[dst, 1, r : r + 4] = (
                uc + (COARSE_RATE * DIFFUSION) * ulap + 0.5 * gain + taus[j - 1, 1, r : r + 4]
            )
        k = phase.base + j

        def pack(f, pair, dst=dst):
            low, high = state[dst, f, 8 + 2 * pair], state[dst, f, 9 + 2 * pair]
            return jnp.where(lane < 16, pltpu.roll(low, 120, 1), pltpu.roll(high, 8, 1))

        if phase.index == 0 and j == phase.steps:
            for f in range(2):
                for pair in range(8):
                    last[f, pair] = pack(f, pair)
        else:

            @pl.when(z_hi == half_of(k))
            def _(k=k, pack=pack):
                for f in range(2):
                    for pair in range(8):
                        emit(k, pair, f, pack(f, pair))


def finish_kernel(start, got, p_out, u_out, made, sems):
    tm, _ = block_index()
    outs = p_out, u_out

    @pl.when(tm == 0)
    def _():
        copies = [pltpu.make_async_copy(start.at[f], outs[f].at[0], sems.at[f]) for f in range(2)]
        for copy in copies:
            copy.start()
        for copy in copies:
            copy.wait()

    @pl.when(tm != 0)
    def _():
        copies = []
        for f in range(2):
            for rp in range(2):
                for b in range(4):
                    parts = transpose_lanes([got[MEMBER[8 * b + j], f, rp] for j in range(8)])
                    for g in range(4):
                        for rr in range(2):
                            at = slice(8 * g, 8 * g + 8), slice(128 * b, 128 * b + 128)
                            made[f, 2 * rp + rr, at[0], at[1]] = parts[2 * g + rr]
                rows = pl.ds(2 * rp, 2)
                copy = pltpu.make_async_copy(
                    made.at[f, rows], outs[f].at[0, rows], sems.at[2 * f + rp]
                )
                copy.start()
                copies.append(copy)
        for copy in copies:
            copy.wait()


VMEM = pl.BlockSpec(memory_space=pltpu.VMEM)
ANY = pl.BlockSpec(memory_space=pl.ANY)


def call(kernel, outs, args, scratch=(), specs=None, grant=40, out_spec=None):
    shapes = [jax.ShapeDtypeStruct(s, jnp.float32) for s in outs]
    return pl.pallas_call(
        kernel,
        out_shape=shapes if len(shapes) > 1 else shapes[0],
        in_specs=specs or [VMEM] * len(args),
        out_specs=[out_spec or VMEM] * len(shapes) if len(shapes) > 1 else out_spec or VMEM,
        scratch_shapes=[pltpu.VMEM(s, jnp.float32) if isinstance(s, tuple) else s for s in scratch],
        cost_estimate=pl.CostEstimate(flops=8, bytes_accessed=8, transcendentals=0),
        compiler_params=pltpu.CompilerParams(vmem_limit_bytes=grant * 1024 * 1024),
    )(*args)


def exchange_rows(payload, axis, pairs):
    odd, even = payload
    got_odd = lax.ppermute(odd, axis, pairs(1))
    got_even = lax.ppermute(even, axis, pairs(0))
    return got_odd, got_even


def local(phase_guess, solute_guess, solute_start, nuclei):
    start = call(
        start_kernel,
        [(2, 4, 32, 512)],
        [nuclei.T, phase_guess, solute_guess, solute_start],
        scratch=[pltpu.SMEM((3, 8), jnp.int32), (2, 4, 32, 512), pltpu.SemaphoreType.DMA((9,))],
        out_spec=ANY,
        specs=[ANY] * 4,
        grant=60,
    )
    even = lax.ppermute(start, "space", space_pairs(0))
    odd = lax.ppermute(start, "space", space_pairs(1))
    packed = call(
        relax_kernel,
        [(32, 2, 2, 8, 128)],
        [start, odd, even],
        scratch=[(2, 12, 48, 512), (2, 12, 48, 512), (2, 4, 32, 512)],
    )
    own = lax.all_to_all(packed, AXES, 0, 0, tiled=True, axis_index_groups=PLANE_GROUPS)
    blank = [(16, 2, 2, 8, 128), (2, 8, 8, 128)]
    shapes = [(4 * blocks, 2, 2, 8, 128) for blocks in (2, 1, 4)]
    near, middle, far, once, *blank = pl.pallas_call(
        cut_kernel,
        out_shape=[jax.ShapeDtypeStruct(s, jnp.float32) for s in shapes]
        + [jax.ShapeDtypeStruct((1,), jnp.int32)]
        + [jax.ShapeDtypeStruct(s, jnp.float32) for s in blank],
        in_specs=[VMEM],
        out_specs=[VMEM, VMEM, VMEM, pl.BlockSpec(memory_space=pltpu.SMEM), ANY, ANY],
        compiler_params=pltpu.CompilerParams(vmem_limit_bytes=40 * 1024 * 1024),
    )(own)
    near = lax.ppermute(near, "tm", ACROSS)
    middle = lax.ppermute(middle, "tm", ACROSS)

    def lanes(phase, known):
        right, left = call(
            lambda *refs: lanes_kernel(phase, *refs), [(4 * phase.steps, 2, 8, 128)] * 2, known
        )
        return [lax.ppermute(right, AXES, RIGHT), lax.ppermute(left, AXES, LEFT)]

    def advance(phase, known, before=(), after=()):
        edges = call(
            lambda *refs: edges_kernel(phase, *refs[len(after) :]),
            [(phase.halo_at[-1], 2, 8, 128)] * 2,
            [*after, *known],
            specs=[ANY] * len(after) + [VMEM] * len(known),
        )
        return call(
            lambda *refs: chain_kernel(phase, *refs),
            [(32, 2, 2, 8, 128)] if phase.index else [(16, 2, 2, 8, 128), (2, 8, 8, 128)],
            [*known, *exchange_rows(edges, AXES, row_pairs), *before],
            scratch=[(2, 2, 32, 8, 128), (phase.steps, 2, 32, 8, 128)],
        )

    known = [own, jnp.concatenate([near, middle])]
    far, _ = lax.optimization_barrier((far, near))
    crossed = lax.ppermute(far, "tm", ACROSS)
    known += lanes(PHASES[0], known)
    before, first = lax.fori_loop(
        0, once[0], lambda i, state: tuple(advance(PHASES[0], known, (), state[1:])), tuple(blank)
    )
    known = [own, crossed, first]
    known += lanes(PHASES[1], known)
    got = advance(PHASES[1], known, [before])
    back = lax.all_to_all(got, AXES, 0, 0, tiled=True, axis_index_groups=PLANE_GROUPS)
    return call(
        finish_kernel,
        [(1, 4, 32, 512)] * 2,
        [start, back],
        scratch=[(2, 4, 32, 512), pltpu.SemaphoreType.DMA((4,))],
        specs=[ANY, VMEM],
        out_spec=ANY,
    )


def solution(mesh):
    return jax.shard_map(
        lambda *args: tuple(local(*args)),
        mesh=mesh,
        in_specs=(
            P("tm", "space", None, None),
            P("tm", "space", None, None),
            P("space", None, None),
            P(),
        ),
        out_specs=(P("tm", "space", None, None), P("tm", "space", None, None)),
        check_vma=False,
    )
```

```python
import jax
import jax.numpy as jnp
from jax import lax
from jax.experimental import pallas as pl
from jax.experimental.pallas import tpu as pltpu
from jax.sharding import PartitionSpec as P

M = 4
FINE_RATE = 0.025
COARSE_RATE = M * FINE_RATE
DIFFUSION = 1.5
WIDTH_SQ = 18.0
AXES = ("tm", "space")


def device(x, y, z_lo, z_hi, core):
    return (y * 4 + z_hi * 2 + core) * 32 + z_lo * 4 + x


def ring_of(x, y, core):
    return 2 * (y * 4 + (3 - x if y & 1 else x)) + core


def place(ring):
    q, core = ring >> 1, ring & 1
    y, x = q >> 2, q & 3
    return (3 - x if y & 1 else x), y, core


PLANES = [(z_lo, z_hi) for z_hi in range(2) for z_lo in range(8)]


def on_ring(ring, plane):
    x, y, core = place(ring % 32)
    return device(x, y, plane[0], plane[1], core)


RING = [ring_of(n % 4, n // 8, (n // 4) % 2) for n in range(32)]
MEMBER = [RING.index(i) for i in range(32)]
PLANE_GROUPS = [[on_ring(i, plane) for i in RING] for plane in PLANES]
RIGHT = [(on_ring(i, plane), on_ring(i + 1, plane)) for plane in PLANES for i in range(32)]
LEFT = [(b, a) for a, b in RIGHT]
ACROSS = [(i, i ^ 2) for i in range(16)]


def row_pairs(parity):
    pairs = []
    for z in range(parity, 16, 2):
        for i in range(32):
            a, b = on_ring(i, (z % 8, z // 8)), on_ring(i, ((z + 1) % 8, (z + 1) // 8 % 2))
            pairs += [(a, b), (b, a)]
    return pairs


def space_pairs(parity):
    pairs = []
    for s in range(parity, 32, 2):
        pairs += [(s, (s + 1) % 32), ((s + 1) % 32, s)]
    return pairs


def growth(pc, uc, pxm, pxp, pym, pyp, pzm, pzp):
    dx, dy, dz = pxp - pxm, pyp - pym, pzp - pzm
    dx, dy, dz = dx * dx, dy * dy, dz * dz
    floor = jnp.maximum(dx + dy + dz, 0.04)
    quartic = (dx * dx + dy * dy + dz * dz) / (floor * floor)
    aniso = 0.85 + 0.2 * quartic
    lap = ((pxp + pxm) + (pyp + pym)) + (pzp + pzm) - 6.0 * pc
    wet = 1.0 - pc * pc
    return aniso * aniso * lap + wet * (pc - 2.0 * uc * wet)


def block_index():
    return lax.axis_index("tm"), lax.axis_index("space")


def start_kernel(nuclei, p_in, u_in, u_start, out, cells, made, sems):
    tm, space = block_index()
    whole = (tm == 0) | (tm == 15)

    def move(f, r, source=None):
        rows = pl.ds(2 * r, 2)
        if source is None:
            return pltpu.make_async_copy(made.at[f, rows], out.at[f, rows], sems.at[2 * f + r])
        return pltpu.make_async_copy(source.at[rows], made.at[f, rows], sems.at[4 + 2 * f + r])

    def through(fields):
        for f, source in fields:
            for r in range(2):
                move(f, r, source).start()
        for f, source in fields:
            for r in range(2):
                move(f, r, source).wait()
                move(f, r).start()

    @pl.when(~whole)
    def _():
        through([(0, p_in.at[0]), (1, u_in.at[0])])

    @pl.when(whole)
    def _():
        n_copy = pltpu.make_async_copy(nuclei, cells, sems.at[8])
        n_copy.start()
        through([(1, u_start)])
        n_copy.wait()
        zs = lax.broadcasted_iota(jnp.int32, (8, 512), 0)
        ys = lax.broadcasted_iota(jnp.int32, (8, 512), 1)
        for g in range(4):
            sides = []
            for n in range(8):
                dy = jnp.abs(ys - cells[2, n])
                dy = jnp.minimum(dy, 512 - dy)
                dz = zs + 8 * g - cells[1, n]
                sides.append(dy * dy + dz * dz)
            for r in range(4):
                best = None
                for n in range(8):
                    dx = jnp.abs(space * 4 + r - cells[0, n])
                    dx = jnp.minimum(dx, 128 - dx)
                    here = sides[n] + dx * dx
                    best = here if best is None else jnp.minimum(best, here)
                b = jnp.exp(-best.astype(jnp.float32) / WIDTH_SQ)
                made[0, r, 8 * g : 8 * g + 8, :] = 2.0 * b - 1.0
        for r in range(2):
            move(0, r).start()

    for f in range(2):
        for r in range(2):
            move(f, r).wait()


def stage_kernel(start, out, sem):
    copy = pltpu.make_async_copy(start, out, sem)
    copy.start()
    copy.wait()


def transpose_lanes(parts):
    slot = lax.broadcasted_iota(jnp.int32, (8, 128), 1) // 16
    parts = [pltpu.roll(part, 16 * a, 1) if a else part for a, part in enumerate(parts)]
    for d in (1, 2, 4):
        move = (slot & d) != 0
        parts = [jnp.where(move, parts[(i + d) % 8], parts[i]) for i in range(8)]
    return [
        pltpu.roll(parts[-j % 8], 128 - 16 * j, 1) if j else parts[0] for j in range(8)
    ]


def relax_kernel(start, odd, even, out, one, two, coarse):
    tm, space = block_index()
    keep = jnp.where((tm == 0) | (tm == 15), 0.0, 1.0)

    def put(buf, f, row, g, value):
        buf[f, row, 8 + 8 * g : 16 + 8 * g, :] = value
        if g == 0:
            buf[f, row, 7:8, :] = value[0:1]
        if g == 3:
            buf[f, row, 40:41, :] = value[7:8]

    def fill(before, after):
        for f in range(2):
            for part, src in enumerate((before, start, after)):
                for r in range(4):
                    for g in range(4):
                        put(one, f, 4 * part + r, g, src[f, r, 8 * g : 8 * g + 8, :])

    @pl.when(space % 2 == 0)
    def _():
        fill(odd, even)

    @pl.when(space % 2 == 1)
    def _():
        fill(even, odd)

    def one_row(src, dst, row, first):
        for g in range(4):
            at = slice(8 + 8 * g, 16 + 8 * g)
            up = slice(9 + 8 * g, 17 + 8 * g)
            down = slice(7 + 8 * g, 15 + 8 * g)
            pc, uc = src[0, row, at, :], src[1, row, at, :]
            rate = growth(
                pc, uc,
                src[0, row - 1, at, :], src[0, row + 1, at, :],
                pltpu.roll(pc, 1, 1), pltpu.roll(pc, 511, 1),
                src[0, row, down, :], src[0, row, up, :],
            )
            ulap = (
                (src[1, row - 1, at, :] + src[1, row + 1, at, :])
                + (pltpu.roll(uc, 1, 1) + pltpu.roll(uc, 511, 1))
                + (src[1, row, down, :] + src[1, row, up, :])
                - 6.0 * uc
            )
            gain = FINE_RATE * rate
            put(dst, 0, row, g, pc + gain)
            put(dst, 1, row, g, uc + (FINE_RATE * DIFFUSION) * ulap + 0.5 * gain)
            if first:
                gain = COARSE_RATE * rate
                coarse[0, row - 4, 8 * g : 8 * g + 8, :] = pc + gain
                coarse[1, row - 4, 8 * g : 8 * g + 8, :] = (
                    uc + (COARSE_RATE * DIFFUSION) * ulap + 0.5 * gain
                )

    def sweep(src, dst, lo, hi, first=False):
        @pl.loop(lo, hi)
        def _(row):
            one_row(src, dst, row, first)

    sweep(one, two, 1, 4)
    sweep(one, two, 4, 8, True)
    sweep(one, two, 8, 11)
    sweep(two, one, 2, 10)
    sweep(one, two, 3, 9)
    sweep(two, one, 4, 8)

    for f in range(2):
        for rp in range(2):
            for b in range(4):
                parts = []
                for g in range(4):
                    for rr in range(2):
                        r = 2 * rp + rr
                        lanes = slice(128 * b, 128 * b + 128)
                        fine = one[f, 4 + r, 8 + 8 * g : 16 + 8 * g, lanes]
                        parts.append(fine - keep * coarse[f, r, 8 * g : 8 * g + 8, lanes])
                for j, part in enumerate(transpose_lanes(parts)):
                    out[MEMBER[8 * b + j], f, rp] = part


STEPS = (6, 8)


class Phase:
    def __init__(self, index):
        self.index = index
        self.steps = STEPS[index]
        self.base = 1 + index * STEPS[0]
        self.halo = [self.steps - j for j in range(self.steps + 1)]
        self.halo_at = [sum(self.halo[:j]) for j in range(self.steps + 2)]


PHASES = Phase(0), Phase(1)


def half_of(k):
    return (k >> 1) & 1


def local_block(k):
    return 2 * (k >> 2) + (k & 1)


def lane32():
    return lax.broadcasted_iota(jnp.int32, (8, 128), 1) % 32


def piece_of(phase, own, other, first, z_hi):
    def get(slot, f, pair):
        x, rp = pair // 2, pair % 2
        if slot == 0 and phase.index:
            return first[f, pair]
        if slot == 0:
            return jnp.where(z_hi == 0, own[x, f, rp], own[28 + x, f, rp])
        k = phase.base + slot - 1
        m = local_block(k)
        sent = m - (4 * phase.index + (1 - phase.index) - half_of(k) * 1)
        return jnp.where(
            half_of(k) == z_hi, own[4 * m + x, f, rp], other[4 * sent + x, f, rp]
        )

    return get


def sent_from(phase, z_hi):
    return 4 * (4 * phase.index + (1 - phase.index) - z_hi)


def split(phase, refs, count):
    if phase.index == 0:
        return refs[0], refs[1], None, *refs[2 : 2 + count]
    return refs[0], refs[1], refs[2], *refs[3 : 3 + count]


def cut_kernel(own, near, middle, far, once, *blank):
    tm, _ = block_index()
    z_hi = (tm // 2) % 2
    at = 4 * (1 - z_hi)
    for out in (near, middle, far):
        out[...] = own[pl.ds(at, out.shape[0])]
        at = at + out.shape[0]
    once[0] = 1


def lanes_kernel(phase, *refs):
    own, other, first, right, left = split(phase, refs, 2)
    tm, _ = block_index()
    get = piece_of(phase, own, other, first, (tm // 2) % 2)
    part = lane32() // 8
    for slot in range(phase.steps):
        for f in range(2):
            for quad in range(4):
                r_edge = l_edge = None
                for q in range(4):
                    if q % 2 == 0:
                        piece = get(slot, f, 2 * quad + q // 2)
                    at = 16 * (q % 2)
                    r_part = pltpu.roll(piece, (8 * q - at - 8) % 128, 1)
                    l_part = pltpu.roll(piece, (8 * q - at + 24) % 128, 1)
                    if q == 0:
                        r_edge, l_edge = r_part, l_part
                    else:
                        r_edge = jnp.where(part == q, r_part, r_edge)
                        l_edge = jnp.where(part == (q + 3) % 4, l_part, l_edge)
                right[4 * slot + quad, f] = r_edge
                left[4 * slot + quad, f] = l_edge


def row_of(phase, get, from_left, from_right):
    part = lane32() // 8

    def row(slot, f, r):
        value = pltpu.roll(get(slot, f, r // 2), 120 if r % 2 else 8, 1)
        if slot == phase.steps:
            return value
        quad, q = 4 * slot + r // 4, r % 4
        halo = jnp.where(part == q, from_left[quad, f], from_right[quad, f])
        if q != 0:
            halo = pltpu.roll(halo, 128 - 8 * q, 1)
        return jnp.where((part == 0) | (part == 3), halo, value)

    return row


def edges_kernel(phase, *refs):
    own, other, first, from_left, from_right, odd, even = split(phase, refs, 4)
    tm, space = block_index()
    get = piece_of(phase, own, other, first, (tm // 2) % 2)
    row = row_of(phase, get, from_left, from_right)
    z_odd = (space // 4) % 2 == 1
    for slot in range(phase.steps):
        n = phase.halo[slot]
        for f in range(2):
            for m in range(n):
                top, bottom = row(slot, f, m), row(slot, f, 16 - n + m)
                odd[phase.halo_at[slot] + m, f] = jnp.where(z_odd, bottom, top)
                even[phase.halo_at[slot] + m, f] = jnp.where(z_odd, top, bottom)


def chain_kernel(phase, *refs):
    if phase.index == 0:
        own, other, first, from_left, from_right, odd, even, out, last, state, taus = split(
            phase, refs, 8
        )
    else:
        own, other, first, from_left, from_right, odd, even, before, out, state, taus = split(
            phase, refs, 8
        )
    tm, space = block_index()
    z_hi = (tm // 2) % 2
    get = piece_of(phase, own, other, first, z_hi)
    row = row_of(phase, get, from_left, from_right)
    z_odd = (space // 4) % 2 == 1
    lane = lane32()
    for slot in range(phase.steps + 1):
        n, at = phase.halo[slot], phase.halo_at[slot]
        for f in range(2):
            put = state.at[0, f] if slot == 0 else taus.at[slot - 1, f]
            for m in range(n):
                put[8 - n + m] = jnp.where(z_odd, even[at + m, f], odd[at + m, f])
                put[24 + m] = jnp.where(z_odd, odd[at + m, f], even[at + m, f])
            for r in range(16):
                put[8 + r] = row(slot, f, r)

    def emit(k, pair, f, piece):
        out[4 * local_block(k) + pair // 2, f, pair % 2] = piece

    if phase.index:
        for i in range(16):
            out[i] = before[i]

    def given():
        for f in range(2):
            for pair in range(8):
                emit(phase.base, pair, f, get(0, f, pair))
                if phase.index == 0:
                    emit(0, pair, f, get(0, f, pair))

    pl.when(z_hi == half_of(phase.base))(given)

    sub = lax.broadcasted_iota(jnp.int32, (4, 8, 128), 1)
    lanes = lax.broadcasted_iota(jnp.int32, (4, 8, 128), 2)
    is_top, is_bottom = sub == 7, sub == 0
    end_up = is_top & (lanes >= 96)
    end_down = is_bottom & (lanes < 32)

    def z_up(v):
        w = jnp.where(is_bottom, pltpu.roll(v, 96, 2), v)
        return jnp.where(end_up, v, pltpu.roll(w, 7, 1))

    def z_down(v):
        w = jnp.where(is_top, pltpu.roll(v, 32, 2), v)
        return jnp.where(end_down, v, pltpu.roll(w, 1, 1))

    for j in range(1, phase.steps + 1):
        src, dst = (j + 1) % 2, j % 2
        lo, hi = 8 - (phase.steps - j), 24 + (phase.steps - j)
        starts = list(range(lo, hi - 3, 4))
        if starts[-1] + 4 < hi:
            starts.append(hi - 4)
        for r in starts:
            pc, uc = state[src, 0, r : r + 4], state[src, 1, r : r + 4]
            rate = growth(
                pc, uc,
                state[src, 0, r - 1 : r + 3], state[src, 0, r + 1 : r + 5],
                pltpu.roll(pc, 1, 2), pltpu.roll(pc, 127, 2),
                z_down(pc), z_up(pc),
            )
            ulap = (
                (state[src, 1, r - 1 : r + 3] + state[src, 1, r + 1 : r + 5])
                + (pltpu.roll(uc, 1, 2) + pltpu.roll(uc, 127, 2))
                + (z_down(uc) + z_up(uc))
                - 6.0 * uc
            )
            gain = COARSE_RATE * rate
            state[dst, 0, r : r + 4] = pc + gain + taus[j - 1, 0, r : r + 4]
            state[dst, 1, r : r + 4] = (
                uc + (COARSE_RATE * DIFFUSION) * ulap + 0.5 * gain + taus[j - 1, 1, r : r + 4]
            )
        k = phase.base + j

        def pack(f, pair, dst=dst):
            low, high = state[dst, f, 8 + 2 * pair], state[dst, f, 9 + 2 * pair]
            return jnp.where(lane < 16, pltpu.roll(low, 120, 1), pltpu.roll(high, 8, 1))

        if phase.index == 0 and j == phase.steps:
            for f in range(2):
                for pair in range(8):
                    last[f, pair] = pack(f, pair)
        else:

            @pl.when(z_hi == half_of(k))
            def _(k=k, pack=pack):
                for f in range(2):
                    for pair in range(8):
                        emit(k, pair, f, pack(f, pair))


def finish_kernel(start, got, p_out, u_out, made, sems):
    tm, _ = block_index()
    outs = p_out, u_out

    @pl.when(tm == 0)
    def _():
        copies = [pltpu.make_async_copy(start.at[f], outs[f].at[0], sems.at[f]) for f in range(2)]
        for copy in copies:
            copy.start()
        for copy in copies:
            copy.wait()

    @pl.when(tm != 0)
    def _():
        copies = []
        for f in range(2):
            for rp in range(2):
                for b in range(4):
                    parts = transpose_lanes([got[MEMBER[8 * b + j], f, rp] for j in range(8)])
                    for g in range(4):
                        for rr in range(2):
                            at = slice(8 * g, 8 * g + 8), slice(128 * b, 128 * b + 128)
                            made[f, 2 * rp + rr, at[0], at[1]] = parts[2 * g + rr]
                rows = pl.ds(2 * rp, 2)
                copy = pltpu.make_async_copy(
                    made.at[f, rows], outs[f].at[0, rows], sems.at[2 * f + rp]
                )
                copy.start()
                copies.append(copy)
        for copy in copies:
            copy.wait()


VMEM = pl.BlockSpec(memory_space=pltpu.VMEM)
ANY = pl.BlockSpec(memory_space=pl.ANY)


def call(kernel, outs, args, scratch=(), specs=None, grant=40, out_spec=None, cost=8):
    shapes = [jax.ShapeDtypeStruct(s, jnp.float32) for s in outs]
    return pl.pallas_call(
        kernel,
        out_shape=shapes if len(shapes) > 1 else shapes[0],
        in_specs=specs or [VMEM] * len(args),
        out_specs=[out_spec or VMEM] * len(shapes) if len(shapes) > 1 else out_spec or VMEM,
        scratch_shapes=[pltpu.VMEM(s, jnp.float32) if isinstance(s, tuple) else s for s in scratch],
        cost_estimate=pl.CostEstimate(flops=8, bytes_accessed=cost, transcendentals=0),
        compiler_params=pltpu.CompilerParams(vmem_limit_bytes=grant * 1024 * 1024),
    )(*args)


def exchange_rows(payload, axis, pairs):
    odd, even = payload
    got_odd = lax.ppermute(odd, axis, pairs(1))
    got_even = lax.ppermute(even, axis, pairs(0))
    return got_odd, got_even


def local(phase_guess, solute_guess, solute_start, nuclei):
    start = call(
        start_kernel,
        [(2, 4, 32, 512)],
        [nuclei.T, phase_guess, solute_guess, solute_start],
        scratch=[pltpu.SMEM((3, 8), jnp.int32), (2, 4, 32, 512), pltpu.SemaphoreType.DMA((9,))],
        out_spec=ANY,
        specs=[ANY] * 4,
        grant=60,
    )
    even = lax.ppermute(start, "space", space_pairs(0))
    odd = lax.ppermute(start, "space", space_pairs(1))
    staged = call(
        stage_kernel,
        [(2, 4, 32, 512)],
        [start],
        scratch=[pltpu.SemaphoreType.DMA],
        specs=[ANY],
        cost=4 * 10**6,
    )
    packed = call(
        relax_kernel,
        [(32, 2, 2, 8, 128)],
        [staged, odd, even],
        scratch=[(2, 12, 48, 512), (2, 12, 48, 512), (2, 4, 32, 512)],
    )
    own = lax.all_to_all(packed, AXES, 0, 0, tiled=True, axis_index_groups=PLANE_GROUPS)
    blank = [(16, 2, 2, 8, 128), (2, 8, 8, 128)]
    shapes = [(4 * blocks, 2, 2, 8, 128) for blocks in (2, 1, 4)]
    near, middle, far, once, *blank = pl.pallas_call(
        cut_kernel,
        out_shape=[jax.ShapeDtypeStruct(s, jnp.float32) for s in shapes]
        + [jax.ShapeDtypeStruct((1,), jnp.int32)]
        + [jax.ShapeDtypeStruct(s, jnp.float32) for s in blank],
        in_specs=[VMEM],
        out_specs=[VMEM, VMEM, VMEM, pl.BlockSpec(memory_space=pltpu.SMEM), ANY, ANY],
        compiler_params=pltpu.CompilerParams(vmem_limit_bytes=40 * 1024 * 1024),
    )(own)
    near = lax.ppermute(near, "tm", ACROSS)
    middle = lax.ppermute(middle, "tm", ACROSS)

    def lanes(phase, known):
        right, left = call(
            lambda *refs: lanes_kernel(phase, *refs), [(4 * phase.steps, 2, 8, 128)] * 2, known
        )
        return [lax.ppermute(right, AXES, RIGHT), lax.ppermute(left, AXES, LEFT)]

    def advance(phase, known, before=(), after=()):
        edges = call(
            lambda *refs: edges_kernel(phase, *refs[len(after) :]),
            [(phase.halo_at[-1], 2, 8, 128)] * 2,
            [*after, *known],
            specs=[ANY] * len(after) + [VMEM] * len(known),
        )
        return call(
            lambda *refs: chain_kernel(phase, *refs),
            [(32, 2, 2, 8, 128)] if phase.index else [(16, 2, 2, 8, 128), (2, 8, 8, 128)],
            [*known, *exchange_rows(edges, AXES, row_pairs), *before],
            scratch=[(2, 2, 32, 8, 128), (phase.steps, 2, 32, 8, 128)],
        )

    known = [own, jnp.concatenate([near, middle])]
    far, _ = lax.optimization_barrier((far, near))
    crossed = lax.ppermute(far, "tm", ACROSS)
    known += lanes(PHASES[0], known)
    before, first = lax.fori_loop(
        0, once[0], lambda i, state: tuple(advance(PHASES[0], known, (), state[1:])), tuple(blank)
    )
    known = [own, crossed, first]
    known += lanes(PHASES[1], known)
    got = advance(PHASES[1], known, [before])
    back = lax.all_to_all(got, AXES, 0, 0, tiled=True, axis_index_groups=PLANE_GROUPS)
    return call(
        finish_kernel,
        [(1, 4, 32, 512)] * 2,
        [start, back],
        scratch=[(2, 4, 32, 512), pltpu.SemaphoreType.DMA((4,))],
        specs=[ANY, VMEM],
        out_spec=ANY,
    )


def solution(mesh):
    return jax.shard_map(
        lambda *args: tuple(local(*args)),
        mesh=mesh,
        in_specs=(
            P("tm", "space", None, None),
            P("tm", "space", None, None),
            P("space", None, None),
            P(),
        ),
        out_specs=(P("tm", "space", None, None), P("tm", "space", None, None)),
        check_vma=False,
    )
```

```python
import jax
import jax.numpy as jnp
from jax import lax
from jax.experimental import pallas as pl
from jax.experimental.pallas import tpu as pltpu
from jax.sharding import PartitionSpec as P

M = 4
FINE_RATE = 0.025
COARSE_RATE = M * FINE_RATE
DIFFUSION = 1.5
WIDTH_SQ = 18.0
AXES = ("tm", "space")


def device(x, y, z_lo, z_hi, core):
    return (y * 4 + z_hi * 2 + core) * 32 + z_lo * 4 + x


def ring_of(x, y, core):
    return 2 * (y * 4 + (3 - x if y & 1 else x)) + core


def place(ring):
    q, core = ring >> 1, ring & 1
    y, x = q >> 2, q & 3
    return (3 - x if y & 1 else x), y, core


PLANES = [(z_lo, z_hi) for z_hi in range(2) for z_lo in range(8)]


def on_ring(ring, plane):
    x, y, core = place(ring % 32)
    return device(x, y, plane[0], plane[1], core)


RING = [ring_of(n % 4, n // 8, (n // 4) % 2) for n in range(32)]
MEMBER = [RING.index(i) for i in range(32)]
PLANE_GROUPS = [[on_ring(i, plane) for i in RING] for plane in PLANES]
ACROSS = [(i, i ^ 2) for i in range(16)]


def lane_pairs(parity):
    pairs = []
    for plane in PLANES:
        for i in range(parity, 32, 2):
            a, b = on_ring(i, plane), on_ring(i + 1, plane)
            pairs += [(a, b), (b, a)]
    return pairs


def row_pairs(parity):
    pairs = []
    for z in range(parity, 16, 2):
        for i in range(32):
            a, b = on_ring(i, (z % 8, z // 8)), on_ring(i, ((z + 1) % 8, (z + 1) // 8 % 2))
            pairs += [(a, b), (b, a)]
    return pairs


def space_pairs(parity):
    pairs = []
    for s in range(parity, 32, 2):
        pairs += [(s, (s + 1) % 32), ((s + 1) % 32, s)]
    return pairs


def growth(pc, uc, pxm, pxp, pym, pyp, pzm, pzp):
    dx, dy, dz = pxp - pxm, pyp - pym, pzp - pzm
    dx, dy, dz = dx * dx, dy * dy, dz * dz
    floor = jnp.maximum(dx + dy + dz, 0.04)
    quartic = (dx * dx + dy * dy + dz * dz) / (floor * floor)
    aniso = 0.85 + 0.2 * quartic
    lap = ((pxp + pxm) + (pyp + pym)) + (pzp + pzm) - 6.0 * pc
    wet = 1.0 - pc * pc
    return aniso * aniso * lap + wet * (pc - 2.0 * uc * wet)


def block_index():
    return lax.axis_index("tm"), lax.axis_index("space")


def start_kernel(nuclei, p_in, u_in, u_start, out, cells, made, sems):
    tm, space = block_index()
    whole = (tm == 0) | (tm == 15)

    def move(f, r, source=None):
        rows = pl.ds(2 * r, 2)
        if source is None:
            return pltpu.make_async_copy(made.at[f, rows], out.at[f, rows], sems.at[2 * f + r])
        return pltpu.make_async_copy(source.at[rows], made.at[f, rows], sems.at[4 + 2 * f + r])

    def through(fields):
        for f, source in fields:
            for r in range(2):
                move(f, r, source).start()
        for f, source in fields:
            for r in range(2):
                move(f, r, source).wait()
                move(f, r).start()

    @pl.when(~whole)
    def _():
        through([(0, p_in.at[0]), (1, u_in.at[0])])

    @pl.when(whole)
    def _():
        n_copy = pltpu.make_async_copy(nuclei, cells, sems.at[8])
        n_copy.start()
        through([(1, u_start)])
        n_copy.wait()
        zs = lax.broadcasted_iota(jnp.int32, (8, 512), 0)
        ys = lax.broadcasted_iota(jnp.int32, (8, 512), 1)
        for g in range(4):
            sides = []
            for n in range(8):
                dy = jnp.abs(ys - cells[2, n])
                dy = jnp.minimum(dy, 512 - dy)
                dz = zs + 8 * g - cells[1, n]
                sides.append(dy * dy + dz * dz)
            for r in range(4):
                best = None
                for n in range(8):
                    dx = jnp.abs(space * 4 + r - cells[0, n])
                    dx = jnp.minimum(dx, 128 - dx)
                    here = sides[n] + dx * dx
                    best = here if best is None else jnp.minimum(best, here)
                b = jnp.exp(-best.astype(jnp.float32) / WIDTH_SQ)
                made[0, r, 8 * g : 8 * g + 8, :] = 2.0 * b - 1.0
        for r in range(2):
            move(0, r).start()

    for f in range(2):
        for r in range(2):
            move(f, r).wait()


def stage_kernel(start, out, sem):
    copy = pltpu.make_async_copy(start, out, sem)
    copy.start()
    copy.wait()


def transpose_lanes(parts):
    slot = lax.broadcasted_iota(jnp.int32, (8, 128), 1) // 16
    parts = [pltpu.roll(part, 16 * a, 1) if a else part for a, part in enumerate(parts)]
    for d in (1, 2, 4):
        move = (slot & d) != 0
        parts = [jnp.where(move, parts[(i + d) % 8], parts[i]) for i in range(8)]
    return [
        pltpu.roll(parts[-j % 8], 128 - 16 * j, 1) if j else parts[0] for j in range(8)
    ]


def relax_kernel(start, odd, even, out, one, two, coarse):
    tm, space = block_index()
    keep = jnp.where((tm == 0) | (tm == 15), 0.0, 1.0)

    def put(buf, f, row, g, value):
        buf[f, row, 8 + 8 * g : 16 + 8 * g, :] = value
        if g == 0:
            buf[f, row, 7:8, :] = value[0:1]
        if g == 3:
            buf[f, row, 40:41, :] = value[7:8]

    def fill(before, after):
        for f in range(2):
            for part, src in enumerate((before, start, after)):
                for r in range(4):
                    for g in range(4):
                        put(one, f, 4 * part + r, g, src[f, r, 8 * g : 8 * g + 8, :])

    @pl.when(space % 2 == 0)
    def _():
        fill(odd, even)

    @pl.when(space % 2 == 1)
    def _():
        fill(even, odd)

    def one_row(src, dst, row, first):
        for g in range(4):
            at = slice(8 + 8 * g, 16 + 8 * g)
            up = slice(9 + 8 * g, 17 + 8 * g)
            down = slice(7 + 8 * g, 15 + 8 * g)
            pc, uc = src[0, row, at, :], src[1, row, at, :]
            rate = growth(
                pc, uc,
                src[0, row - 1, at, :], src[0, row + 1, at, :],
                pltpu.roll(pc, 1, 1), pltpu.roll(pc, 511, 1),
                src[0, row, down, :], src[0, row, up, :],
            )
            ulap = (
                (src[1, row - 1, at, :] + src[1, row + 1, at, :])
                + (pltpu.roll(uc, 1, 1) + pltpu.roll(uc, 511, 1))
                + (src[1, row, down, :] + src[1, row, up, :])
                - 6.0 * uc
            )
            gain = FINE_RATE * rate
            put(dst, 0, row, g, pc + gain)
            put(dst, 1, row, g, uc + (FINE_RATE * DIFFUSION) * ulap + 0.5 * gain)
            if first:
                gain = COARSE_RATE * rate
                coarse[0, row - 4, 8 * g : 8 * g + 8, :] = pc + gain
                coarse[1, row - 4, 8 * g : 8 * g + 8, :] = (
                    uc + (COARSE_RATE * DIFFUSION) * ulap + 0.5 * gain
                )

    def sweep(src, dst, lo, hi, first=False):
        @pl.loop(lo, hi)
        def _(row):
            one_row(src, dst, row, first)

    sweep(one, two, 1, 4)
    sweep(one, two, 4, 8, True)
    sweep(one, two, 8, 11)
    sweep(two, one, 2, 10)
    sweep(one, two, 3, 9)
    sweep(two, one, 4, 8)

    for f in range(2):
        for rp in range(2):
            for b in range(4):
                parts = []
                for g in range(4):
                    for rr in range(2):
                        r = 2 * rp + rr
                        lanes = slice(128 * b, 128 * b + 128)
                        fine = one[f, 4 + r, 8 + 8 * g : 16 + 8 * g, lanes]
                        parts.append(fine - keep * coarse[f, r, 8 * g : 8 * g + 8, lanes])
                for j, part in enumerate(transpose_lanes(parts)):
                    out[MEMBER[8 * b + j], f, rp] = part


STEPS = (6, 8)


class Phase:
    def __init__(self, index):
        self.index = index
        self.steps = STEPS[index]
        self.base = 1 + index * STEPS[0]
        self.halo = [self.steps - j for j in range(self.steps + 1)]
        self.halo_at = [sum(self.halo[:j]) for j in range(self.steps + 2)]


PHASES = Phase(0), Phase(1)


def half_of(k):
    return (k >> 1) & 1


def local_block(k):
    return 2 * (k >> 2) + (k & 1)


def lane32():
    return lax.broadcasted_iota(jnp.int32, (8, 128), 1) % 32


def piece_of(phase, own, other, first, z_hi):
    def get(slot, f, pair):
        x, rp = pair // 2, pair % 2
        if slot == 0 and phase.index:
            return first[f, pair]
        if slot == 0:
            return jnp.where(z_hi == 0, own[x, f, rp], own[28 + x, f, rp])
        k = phase.base + slot - 1
        m = local_block(k)
        sent = m - (4 * phase.index + (1 - phase.index) - half_of(k) * 1)
        return jnp.where(
            half_of(k) == z_hi, own[4 * m + x, f, rp], other[4 * sent + x, f, rp]
        )

    return get


def sent_from(phase, z_hi):
    return 4 * (4 * phase.index + (1 - phase.index) - z_hi)


def split(phase, refs, count):
    if phase.index == 0:
        return refs[0], refs[1], None, *refs[2 : 2 + count]
    return refs[0], refs[1], refs[2], *refs[3 : 3 + count]


def cut_kernel(own, near, middle, far, once, *blank):
    tm, _ = block_index()
    z_hi = (tm // 2) % 2
    at = 4 * (1 - z_hi)
    for out in (near, middle, far):
        out[...] = own[pl.ds(at, out.shape[0])]
        at = at + out.shape[0]
    once[0] = 1


def lanes_kernel(phase, *refs):
    own, other, first, odd, even = split(phase, refs, 2)
    tm, _ = block_index()
    get = piece_of(phase, own, other, first, (tm // 2) % 2)
    part = lane32() // 8
    is_odd = tm % 2 == 1
    for slot in range(phase.steps):
        for f in range(2):
            for quad in range(4):
                r_edge = l_edge = None
                for q in range(4):
                    if q % 2 == 0:
                        piece = get(slot, f, 2 * quad + q // 2)
                    at = 16 * (q % 2)
                    r_part = pltpu.roll(piece, (8 * q - at - 8) % 128, 1)
                    l_part = pltpu.roll(piece, (8 * q - at + 24) % 128, 1)
                    if q == 0:
                        r_edge, l_edge = r_part, l_part
                    else:
                        r_edge = jnp.where(part == q, r_part, r_edge)
                        l_edge = jnp.where(part == (q + 3) % 4, l_part, l_edge)
                odd[4 * slot + quad, f] = jnp.where(is_odd, r_edge, l_edge)
                even[4 * slot + quad, f] = jnp.where(is_odd, l_edge, r_edge)


def row_of(phase, get, odd, even, is_odd):
    part = lane32() // 8

    def row(slot, f, r):
        value = pltpu.roll(get(slot, f, r // 2), 120 if r % 2 else 8, 1)
        if slot == phase.steps:
            return value
        quad, q = 4 * slot + r // 4, r % 4
        halo = jnp.where((part == q) ^ is_odd, odd[quad, f], even[quad, f])
        if q != 0:
            halo = pltpu.roll(halo, 128 - 8 * q, 1)
        return jnp.where((part == 0) | (part == 3), halo, value)

    return row


def edges_kernel(phase, *refs):
    own, other, first, lanes_odd, lanes_even, odd, even = split(phase, refs, 4)
    tm, space = block_index()
    get = piece_of(phase, own, other, first, (tm // 2) % 2)
    row = row_of(phase, get, lanes_odd, lanes_even, tm % 2 == 1)
    z_odd = (space // 4) % 2 == 1
    for slot in range(phase.steps):
        n = phase.halo[slot]
        for f in range(2):
            for m in range(n):
                top, bottom = row(slot, f, m), row(slot, f, 16 - n + m)
                odd[phase.halo_at[slot] + m, f] = jnp.where(z_odd, bottom, top)
                even[phase.halo_at[slot] + m, f] = jnp.where(z_odd, top, bottom)


def chain_kernel(phase, *refs):
    if phase.index == 0:
        own, other, first, lanes_odd, lanes_even, odd, even, out, last, state, taus = split(
            phase, refs, 8
        )
    else:
        own, other, first, lanes_odd, lanes_even, odd, even, before, out, state, taus = split(
            phase, refs, 8
        )
    tm, space = block_index()
    z_hi = (tm // 2) % 2
    get = piece_of(phase, own, other, first, z_hi)
    row = row_of(phase, get, lanes_odd, lanes_even, tm % 2 == 1)
    z_odd = (space // 4) % 2 == 1
    lane = lane32()
    for slot in range(phase.steps + 1):
        n, at = phase.halo[slot], phase.halo_at[slot]
        for f in range(2):
            put = state.at[0, f] if slot == 0 else taus.at[slot - 1, f]
            for m in range(n):
                put[8 - n + m] = jnp.where(z_odd, even[at + m, f], odd[at + m, f])
                put[24 + m] = jnp.where(z_odd, odd[at + m, f], even[at + m, f])
            for r in range(16):
                put[8 + r] = row(slot, f, r)

    def emit(k, pair, f, piece):
        out[4 * local_block(k) + pair // 2, f, pair % 2] = piece

    if phase.index:
        for i in range(16):
            out[i] = before[i]

    def given():
        for f in range(2):
            for pair in range(8):
                emit(phase.base, pair, f, get(0, f, pair))
                if phase.index == 0:
                    emit(0, pair, f, get(0, f, pair))

    pl.when(z_hi == half_of(phase.base))(given)

    sub = lax.broadcasted_iota(jnp.int32, (4, 8, 128), 1)
    lanes = lax.broadcasted_iota(jnp.int32, (4, 8, 128), 2)
    is_top, is_bottom = sub == 7, sub == 0
    end_up = is_top & (lanes >= 96)
    end_down = is_bottom & (lanes < 32)

    def z_up(v):
        w = jnp.where(is_bottom, pltpu.roll(v, 96, 2), v)
        return jnp.where(end_up, v, pltpu.roll(w, 7, 1))

    def z_down(v):
        w = jnp.where(is_top, pltpu.roll(v, 32, 2), v)
        return jnp.where(end_down, v, pltpu.roll(w, 1, 1))

    for j in range(1, phase.steps + 1):
        src, dst = (j + 1) % 2, j % 2
        lo, hi = 8 - (phase.steps - j), 24 + (phase.steps - j)
        starts = list(range(lo, hi - 3, 4))
        if starts[-1] + 4 < hi:
            starts.append(hi - 4)
        for r in starts:
            pc, uc = state[src, 0, r : r + 4], state[src, 1, r : r + 4]
            rate = growth(
                pc, uc,
                state[src, 0, r - 1 : r + 3], state[src, 0, r + 1 : r + 5],
                pltpu.roll(pc, 1, 2), pltpu.roll(pc, 127, 2),
                z_down(pc), z_up(pc),
            )
            ulap = (
                (state[src, 1, r - 1 : r + 3] + state[src, 1, r + 1 : r + 5])
                + (pltpu.roll(uc, 1, 2) + pltpu.roll(uc, 127, 2))
                + (z_down(uc) + z_up(uc))
                - 6.0 * uc
            )
            gain = COARSE_RATE * rate
            state[dst, 0, r : r + 4] = pc + gain + taus[j - 1, 0, r : r + 4]
            state[dst, 1, r : r + 4] = (
                uc + (COARSE_RATE * DIFFUSION) * ulap + 0.5 * gain + taus[j - 1, 1, r : r + 4]
            )
        k = phase.base + j

        def pack(f, pair, dst=dst):
            low, high = state[dst, f, 8 + 2 * pair], state[dst, f, 9 + 2 * pair]
            return jnp.where(lane < 16, pltpu.roll(low, 120, 1), pltpu.roll(high, 8, 1))

        if phase.index == 0 and j == phase.steps:
            for f in range(2):
                for pair in range(8):
                    last[f, pair] = pack(f, pair)
        else:

            @pl.when(z_hi == half_of(k))
            def _(k=k, pack=pack):
                for f in range(2):
                    for pair in range(8):
                        emit(k, pair, f, pack(f, pair))


def finish_kernel(start, got, p_out, u_out, made, sems):
    tm, _ = block_index()
    outs = p_out, u_out

    @pl.when(tm == 0)
    def _():
        copies = [pltpu.make_async_copy(start.at[f], outs[f].at[0], sems.at[f]) for f in range(2)]
        for copy in copies:
            copy.start()
        for copy in copies:
            copy.wait()

    @pl.when(tm != 0)
    def _():
        copies = []
        for f in range(2):
            for rp in range(2):
                for b in range(4):
                    parts = transpose_lanes([got[MEMBER[8 * b + j], f, rp] for j in range(8)])
                    for g in range(4):
                        for rr in range(2):
                            at = slice(8 * g, 8 * g + 8), slice(128 * b, 128 * b + 128)
                            made[f, 2 * rp + rr, at[0], at[1]] = parts[2 * g + rr]
                rows = pl.ds(2 * rp, 2)
                copy = pltpu.make_async_copy(
                    made.at[f, rows], outs[f].at[0, rows], sems.at[2 * f + rp]
                )
                copy.start()
                copies.append(copy)
        for copy in copies:
            copy.wait()


VMEM = pl.BlockSpec(memory_space=pltpu.VMEM)
ANY = pl.BlockSpec(memory_space=pl.ANY)


def call(kernel, outs, args, scratch=(), specs=None, grant=40, out_spec=None, cost=8):
    shapes = [jax.ShapeDtypeStruct(s, jnp.float32) for s in outs]
    return pl.pallas_call(
        kernel,
        out_shape=shapes if len(shapes) > 1 else shapes[0],
        in_specs=specs or [VMEM] * len(args),
        out_specs=[out_spec or VMEM] * len(shapes) if len(shapes) > 1 else out_spec or VMEM,
        scratch_shapes=[pltpu.VMEM(s, jnp.float32) if isinstance(s, tuple) else s for s in scratch],
        cost_estimate=pl.CostEstimate(flops=8, bytes_accessed=cost, transcendentals=0),
        compiler_params=pltpu.CompilerParams(vmem_limit_bytes=grant * 1024 * 1024),
    )(*args)


def exchange(payload, axis, pairs):
    odd, even = payload
    got_odd = lax.ppermute(odd, axis, pairs(1))
    got_even = lax.ppermute(even, axis, pairs(0))
    return got_odd, got_even


def local(phase_guess, solute_guess, solute_start, nuclei):
    start = call(
        start_kernel,
        [(2, 4, 32, 512)],
        [nuclei.T, phase_guess, solute_guess, solute_start],
        scratch=[pltpu.SMEM((3, 8), jnp.int32), (2, 4, 32, 512), pltpu.SemaphoreType.DMA((9,))],
        out_spec=ANY,
        specs=[ANY] * 4,
        grant=60,
    )
    even = lax.ppermute(start, "space", space_pairs(0))
    odd = lax.ppermute(start, "space", space_pairs(1))
    staged = call(
        stage_kernel,
        [(2, 4, 32, 512)],
        [start],
        scratch=[pltpu.SemaphoreType.DMA],
        specs=[ANY],
        cost=4 * 10**6,
    )
    packed = call(
        relax_kernel,
        [(32, 2, 2, 8, 128)],
        [staged, odd, even],
        scratch=[(2, 12, 48, 512), (2, 12, 48, 512), (2, 4, 32, 512)],
    )
    own = lax.all_to_all(packed, AXES, 0, 0, tiled=True, axis_index_groups=PLANE_GROUPS)
    blank = [(16, 2, 2, 8, 128), (2, 8, 8, 128)]
    shapes = [(4 * blocks, 2, 2, 8, 128) for blocks in (2, 1, 4)]
    near, middle, far, once, *blank = pl.pallas_call(
        cut_kernel,
        out_shape=[jax.ShapeDtypeStruct(s, jnp.float32) for s in shapes]
        + [jax.ShapeDtypeStruct((1,), jnp.int32)]
        + [jax.ShapeDtypeStruct(s, jnp.float32) for s in blank],
        in_specs=[VMEM],
        out_specs=[VMEM, VMEM, VMEM, pl.BlockSpec(memory_space=pltpu.SMEM), ANY, ANY],
        compiler_params=pltpu.CompilerParams(vmem_limit_bytes=40 * 1024 * 1024),
    )(own)
    near = lax.ppermute(near, "tm", ACROSS)
    middle = lax.ppermute(middle, "tm", ACROSS)

    def lanes(phase, known):
        edges = call(
            lambda *refs: lanes_kernel(phase, *refs), [(4 * phase.steps, 2, 8, 128)] * 2, known
        )
        return exchange(edges, AXES, lane_pairs)

    def advance(phase, known, before=(), after=()):
        edges = call(
            lambda *refs: edges_kernel(phase, *refs[len(after) :]),
            [(phase.halo_at[-1], 2, 8, 128)] * 2,
            [*after, *known],
            specs=[ANY] * len(after) + [VMEM] * len(known),
        )
        return call(
            lambda *refs: chain_kernel(phase, *refs),
            [(32, 2, 2, 8, 128)] if phase.index else [(16, 2, 2, 8, 128), (2, 8, 8, 128)],
            [*known, *exchange(edges, AXES, row_pairs), *before],
            scratch=[(2, 2, 32, 8, 128), (phase.steps, 2, 32, 8, 128)],
        )

    known = [own, jnp.concatenate([near, middle])]
    far, _ = lax.optimization_barrier((far, near))
    crossed = lax.ppermute(far, "tm", ACROSS)
    known += lanes(PHASES[0], known)
    before, first = lax.fori_loop(
        0, once[0], lambda i, state: tuple(advance(PHASES[0], known, (), state[1:])), tuple(blank)
    )
    known = [own, crossed, first]
    known += lanes(PHASES[1], known)
    got = advance(PHASES[1], known, [before])
    back = lax.all_to_all(got, AXES, 0, 0, tiled=True, axis_index_groups=PLANE_GROUPS)
    return call(
        finish_kernel,
        [(1, 4, 32, 512)] * 2,
        [start, back],
        scratch=[(2, 4, 32, 512), pltpu.SemaphoreType.DMA((4,))],
        specs=[ANY, VMEM],
        out_spec=ANY,
    )


def solution(mesh):
    return jax.shard_map(
        lambda *args: tuple(local(*args)),
        mesh=mesh,
        in_specs=(
            P("tm", "space", None, None),
            P("tm", "space", None, None),
            P("space", None, None),
            P(),
        ),
        out_specs=(P("tm", "space", None, None), P("tm", "space", None, None)),
        check_vma=False,
    )
```

```python
import jax
import jax.numpy as jnp
from jax import lax
from jax.experimental import pallas as pl
from jax.experimental.pallas import tpu as pltpu
from jax.sharding import PartitionSpec as P

M = 4
FINE_RATE = 0.025
COARSE_RATE = M * FINE_RATE
DIFFUSION = 1.5
WIDTH_SQ = 18.0
AXES = ("tm", "space")


def device(x, y, z_lo, z_hi, core):
    return (y * 4 + z_hi * 2 + core) * 32 + z_lo * 4 + x


def ring_of(x, y, core):
    return 2 * (y * 4 + (3 - x if y & 1 else x)) + core


def place(ring):
    q, core = ring >> 1, ring & 1
    y, x = q >> 2, q & 3
    return (3 - x if y & 1 else x), y, core


PLANES = [(z_lo, z_hi) for z_hi in range(2) for z_lo in range(8)]


def on_ring(ring, plane):
    x, y, core = place(ring % 32)
    return device(x, y, plane[0], plane[1], core)


RING = [ring_of(n % 4, n // 8, (n // 4) % 2) for n in range(32)]
MEMBER = [RING.index(i) for i in range(32)]
PLANE_GROUPS = [[on_ring(i, plane) for i in RING] for plane in PLANES]
ACROSS = [(i, i ^ 2) for i in range(16)]


def lane_pairs(parity):
    pairs = []
    for plane in PLANES:
        for i in range(parity, 32, 2):
            a, b = on_ring(i, plane), on_ring(i + 1, plane)
            pairs += [(a, b), (b, a)]
    return pairs


def row_pairs(parity):
    pairs = []
    for z in range(parity, 16, 2):
        for i in range(32):
            a, b = on_ring(i, (z % 8, z // 8)), on_ring(i, ((z + 1) % 8, (z + 1) // 8 % 2))
            pairs += [(a, b), (b, a)]
    return pairs


def space_pairs(parity):
    pairs = []
    for s in range(parity, 32, 2):
        pairs += [(s, (s + 1) % 32), ((s + 1) % 32, s)]
    return pairs


def growth(pc, uc, pxm, pxp, pym, pyp, pzm, pzp):
    dx, dy, dz = pxp - pxm, pyp - pym, pzp - pzm
    dx, dy, dz = dx * dx, dy * dy, dz * dz
    floor = jnp.maximum(dx + dy + dz, 0.04)
    quartic = (dx * dx + dy * dy + dz * dz) / (floor * floor)
    aniso = 0.85 + 0.2 * quartic
    lap = ((pxp + pxm) + (pyp + pym)) + (pzp + pzm) - 6.0 * pc
    wet = 1.0 - pc * pc
    return aniso * aniso * lap + wet * (pc - 2.0 * uc * wet)


def block_index():
    return lax.axis_index("tm"), lax.axis_index("space")


def start_kernel(nuclei, p_in, u_in, u_start, out, cells, made, sems):
    tm, space = block_index()
    whole = (tm == 0) | (tm == 15)

    def move(f, r, source=None):
        rows = pl.ds(2 * r, 2)
        if source is None:
            return pltpu.make_async_copy(made.at[f, rows], out.at[f, rows], sems.at[2 * f + r])
        return pltpu.make_async_copy(source.at[rows], made.at[f, rows], sems.at[4 + 2 * f + r])

    def through(fields):
        for f, source in fields:
            for r in range(2):
                move(f, r, source).start()
        for f, source in fields:
            for r in range(2):
                move(f, r, source).wait()
                move(f, r).start()

    @pl.when(~whole)
    def _():
        through([(0, p_in.at[0]), (1, u_in.at[0])])

    @pl.when(whole)
    def _():
        n_copy = pltpu.make_async_copy(nuclei, cells, sems.at[8])
        n_copy.start()
        through([(1, u_start)])
        n_copy.wait()
        zs = lax.broadcasted_iota(jnp.int32, (8, 512), 0)
        ys = lax.broadcasted_iota(jnp.int32, (8, 512), 1)
        for g in range(4):
            sides = []
            for n in range(8):
                dy = jnp.abs(ys - cells[2, n])
                dy = jnp.minimum(dy, 512 - dy)
                dz = zs + 8 * g - cells[1, n]
                sides.append(dy * dy + dz * dz)
            for r in range(4):
                best = None
                for n in range(8):
                    dx = jnp.abs(space * 4 + r - cells[0, n])
                    dx = jnp.minimum(dx, 128 - dx)
                    here = sides[n] + dx * dx
                    best = here if best is None else jnp.minimum(best, here)
                b = jnp.exp(-best.astype(jnp.float32) / WIDTH_SQ)
                made[0, r, 8 * g : 8 * g + 8, :] = 2.0 * b - 1.0
        for r in range(2):
            move(0, r).start()

    for f in range(2):
        for r in range(2):
            move(f, r).wait()


def stage_kernel(start, out, sem):
    copy = pltpu.make_async_copy(start, out, sem)
    copy.start()
    copy.wait()


def transpose_lanes(parts):
    slot = lax.broadcasted_iota(jnp.int32, (8, 128), 1) // 16
    parts = [pltpu.roll(part, 16 * a, 1) if a else part for a, part in enumerate(parts)]
    for d in (1, 2, 4):
        move = (slot & d) != 0
        parts = [jnp.where(move, parts[(i + d) % 8], parts[i]) for i in range(8)]
    return [
        pltpu.roll(parts[-j % 8], 128 - 16 * j, 1) if j else parts[0] for j in range(8)
    ]


def relax_kernel(start, odd, even, out, one, two, coarse):
    tm, space = block_index()
    keep = jnp.where((tm == 0) | (tm == 15), 0.0, 1.0)

    def put(buf, f, row, g, value):
        buf[f, row, 8 + 8 * g : 16 + 8 * g, :] = value
        if g == 0:
            buf[f, row, 7:8, :] = value[0:1]
        if g == 3:
            buf[f, row, 40:41, :] = value[7:8]

    def fill(before, after):
        for f in range(2):
            for part, src in enumerate((before, start, after)):
                for r in range(4):
                    for g in range(4):
                        put(one, f, 4 * part + r, g, src[f, r, 8 * g : 8 * g + 8, :])

    @pl.when(space % 2 == 0)
    def _():
        fill(odd, even)

    @pl.when(space % 2 == 1)
    def _():
        fill(even, odd)

    def one_row(src, dst, row, first):
        for g in range(4):
            at = slice(8 + 8 * g, 16 + 8 * g)
            up = slice(9 + 8 * g, 17 + 8 * g)
            down = slice(7 + 8 * g, 15 + 8 * g)
            pc, uc = src[0, row, at, :], src[1, row, at, :]
            rate = growth(
                pc, uc,
                src[0, row - 1, at, :], src[0, row + 1, at, :],
                pltpu.roll(pc, 1, 1), pltpu.roll(pc, 511, 1),
                src[0, row, down, :], src[0, row, up, :],
            )
            ulap = (
                (src[1, row - 1, at, :] + src[1, row + 1, at, :])
                + (pltpu.roll(uc, 1, 1) + pltpu.roll(uc, 511, 1))
                + (src[1, row, down, :] + src[1, row, up, :])
                - 6.0 * uc
            )
            gain = FINE_RATE * rate
            put(dst, 0, row, g, pc + gain)
            put(dst, 1, row, g, uc + (FINE_RATE * DIFFUSION) * ulap + 0.5 * gain)
            if first:
                gain = COARSE_RATE * rate
                coarse[0, row - 4, 8 * g : 8 * g + 8, :] = pc + gain
                coarse[1, row - 4, 8 * g : 8 * g + 8, :] = (
                    uc + (COARSE_RATE * DIFFUSION) * ulap + 0.5 * gain
                )

    def sweep(src, dst, lo, hi, first=False):
        @pl.loop(lo, hi)
        def _(row):
            one_row(src, dst, row, first)

    sweep(one, two, 1, 4)
    sweep(one, two, 4, 8, True)
    sweep(one, two, 8, 11)
    sweep(two, one, 2, 10)
    sweep(one, two, 3, 9)
    sweep(two, one, 4, 8)

    for f in range(2):
        for rp in range(2):
            for b in range(4):
                parts = []
                for g in range(4):
                    for rr in range(2):
                        r = 2 * rp + rr
                        lanes = slice(128 * b, 128 * b + 128)
                        fine = one[f, 4 + r, 8 + 8 * g : 16 + 8 * g, lanes]
                        parts.append(fine - keep * coarse[f, r, 8 * g : 8 * g + 8, lanes])
                for j, part in enumerate(transpose_lanes(parts)):
                    out[MEMBER[8 * b + j], f, rp] = part


STEPS = (6, 8)


class Phase:
    def __init__(self, index):
        self.index = index
        self.steps = STEPS[index]
        self.base = 1 + index * STEPS[0]
        self.halo = [self.steps - j for j in range(self.steps + 1)]
        self.halo_at = [sum(self.halo[:j]) for j in range(self.steps + 2)]


PHASES = Phase(0), Phase(1)


def half_of(k):
    return (k >> 1) & 1


def local_block(k):
    return 2 * (k >> 2) + (k & 1)


def lane32():
    return lax.broadcasted_iota(jnp.int32, (8, 128), 1) % 32


def piece_of(phase, own, other, first, z_hi):
    def get(slot, f, pair):
        x, rp = pair // 2, pair % 2
        if slot == 0 and phase.index:
            return first[f, pair]
        if slot == 0:
            return jnp.where(z_hi == 0, own[x, f, rp], own[28 + x, f, rp])
        k = phase.base + slot - 1
        m = local_block(k)
        sent = m - (4 * phase.index + (1 - phase.index) - half_of(k) * 1)
        return jnp.where(
            half_of(k) == z_hi, own[4 * m + x, f, rp], other[4 * sent + x, f, rp]
        )

    return get


def sent_from(phase, z_hi):
    return 4 * (4 * phase.index + (1 - phase.index) - z_hi)


def split(phase, refs, count):
    if phase.index == 0:
        return refs[0], refs[1], None, *refs[2 : 2 + count]
    return refs[0], refs[1], refs[2], *refs[3 : 3 + count]


def cut_kernel(own, near, middle, far, once, *blank):
    tm, _ = block_index()
    z_hi = (tm // 2) % 2
    at = 4 * (1 - z_hi)
    for out in (near, middle, far):
        out[...] = own[pl.ds(at, out.shape[0])]
        at = at + out.shape[0]
    once[0] = 1


def lanes_kernel(phase, *refs):
    own, other, first, odd, even = split(phase, refs, 2)
    tm, _ = block_index()
    get = piece_of(phase, own, other, first, (tm // 2) % 2)
    part = lane32() // 8
    is_odd = tm % 2 == 1
    for slot in range(phase.steps):
        for f in range(2):
            for quad in range(4):
                r_edge = l_edge = None
                for q in range(4):
                    if q % 2 == 0:
                        piece = get(slot, f, 2 * quad + q // 2)
                    at = 16 * (q % 2)
                    r_part = pltpu.roll(piece, (8 * q - at - 8) % 128, 1)
                    l_part = pltpu.roll(piece, (8 * q - at + 24) % 128, 1)
                    if q == 0:
                        r_edge, l_edge = r_part, l_part
                    else:
                        r_edge = jnp.where(part == q, r_part, r_edge)
                        l_edge = jnp.where(part == (q + 3) % 4, l_part, l_edge)
                odd[4 * slot + quad, f] = jnp.where(is_odd, r_edge, l_edge)
                even[4 * slot + quad, f] = jnp.where(is_odd, l_edge, r_edge)


def row_of(phase, get, odd, even, is_odd):
    part = lane32() // 8

    def row(slot, f, r):
        value = pltpu.roll(get(slot, f, r // 2), 120 if r % 2 else 8, 1)
        if slot == phase.steps:
            return value
        quad, q = 4 * slot + r // 4, r % 4
        halo = jnp.where((part == q) ^ is_odd, odd[quad, f], even[quad, f])
        if q != 0:
            halo = pltpu.roll(halo, 128 - 8 * q, 1)
        return jnp.where((part == 0) | (part == 3), halo, value)

    return row


def edges_kernel(phase, *refs):
    own, other, first, lanes_odd, lanes_even, odd, even = split(phase, refs, 4)
    tm, space = block_index()
    get = piece_of(phase, own, other, first, (tm // 2) % 2)
    row = row_of(phase, get, lanes_odd, lanes_even, tm % 2 == 1)
    z_odd = (space // 4) % 2 == 1
    for slot in range(phase.steps):
        n = phase.halo[slot]
        for f in range(2):
            for m in range(n):
                top, bottom = row(slot, f, m), row(slot, f, 16 - n + m)
                odd[phase.halo_at[slot] + m, f] = jnp.where(z_odd, bottom, top)
                even[phase.halo_at[slot] + m, f] = jnp.where(z_odd, top, bottom)


def chain_kernel(phase, *refs):
    if phase.index == 0:
        own, other, first, lanes_odd, lanes_even, odd, even, out, last, state, taus = split(
            phase, refs, 8
        )
    else:
        own, other, first, lanes_odd, lanes_even, odd, even, before, out, state, taus = split(
            phase, refs, 8
        )
    tm, space = block_index()
    z_hi = (tm // 2) % 2
    get = piece_of(phase, own, other, first, z_hi)
    row = row_of(phase, get, lanes_odd, lanes_even, tm % 2 == 1)
    z_odd = (space // 4) % 2 == 1
    lane = lane32()
    for slot in range(phase.steps + 1):
        n, at = phase.halo[slot], phase.halo_at[slot]
        for f in range(2):
            put = state.at[0, f] if slot == 0 else taus.at[slot - 1, f]
            for m in range(n):
                put[8 - n + m] = jnp.where(z_odd, even[at + m, f], odd[at + m, f])
                put[24 + m] = jnp.where(z_odd, odd[at + m, f], even[at + m, f])
            for r in range(16):
                put[8 + r] = row(slot, f, r)

    def emit(k, pair, f, piece):
        out[4 * local_block(k) + pair // 2, f, pair % 2] = piece

    if phase.index:
        for i in range(16):
            out[i] = before[i]

    def given():
        for f in range(2):
            for pair in range(8):
                emit(phase.base, pair, f, get(0, f, pair))
                if phase.index == 0:
                    emit(0, pair, f, get(0, f, pair))

    pl.when(z_hi == half_of(phase.base))(given)

    sub = lax.broadcasted_iota(jnp.int32, (4, 8, 128), 1)
    lanes = lax.broadcasted_iota(jnp.int32, (4, 8, 128), 2)
    is_top, is_bottom = sub == 7, sub == 0
    end_up = is_top & (lanes >= 96)
    end_down = is_bottom & (lanes < 32)

    def z_next(p, u, lanes_on, near, far, by, end):
        u_turned = pltpu.roll(u, by, 1)
        crossed = pltpu.roll(jnp.where(far, u_turned, p), lanes_on, 2)
        p_turned = pltpu.roll(jnp.where(near, crossed, p), by, 1)
        return jnp.where(end, p, p_turned), jnp.where(end, u, jnp.where(far, crossed, u_turned))

    for j in range(1, phase.steps + 1):
        src, dst = (j + 1) % 2, j % 2
        lo, hi = 8 - (phase.steps - j), 24 + (phase.steps - j)
        starts = list(range(lo, hi - 3, 4))
        if starts[-1] + 4 < hi:
            starts.append(hi - 4)
        for r in starts:
            pc, uc = state[src, 0, r : r + 4], state[src, 1, r : r + 4]
            p_up, u_up = z_next(pc, uc, 96, is_bottom, is_top, 7, end_up)
            p_down, u_down = z_next(pc, uc, 32, is_top, is_bottom, 1, end_down)
            rate = growth(
                pc, uc,
                state[src, 0, r - 1 : r + 3], state[src, 0, r + 1 : r + 5],
                pltpu.roll(pc, 1, 2), pltpu.roll(pc, 127, 2),
                p_down, p_up,
            )
            ulap = (
                (state[src, 1, r - 1 : r + 3] + state[src, 1, r + 1 : r + 5])
                + (pltpu.roll(uc, 1, 2) + pltpu.roll(uc, 127, 2))
                + (u_down + u_up)
                - 6.0 * uc
            )
            gain = COARSE_RATE * rate
            state[dst, 0, r : r + 4] = pc + gain + taus[j - 1, 0, r : r + 4]
            state[dst, 1, r : r + 4] = (
                uc + (COARSE_RATE * DIFFUSION) * ulap + 0.5 * gain + taus[j - 1, 1, r : r + 4]
            )
        k = phase.base + j

        def pack(f, pair, dst=dst):
            low, high = state[dst, f, 8 + 2 * pair], state[dst, f, 9 + 2 * pair]
            return jnp.where(lane < 16, pltpu.roll(low, 120, 1), pltpu.roll(high, 8, 1))

        if phase.index == 0 and j == phase.steps:
            for f in range(2):
                for pair in range(8):
                    last[f, pair] = pack(f, pair)
        else:

            @pl.when(z_hi == half_of(k))
            def _(k=k, pack=pack):
                for f in range(2):
                    for pair in range(8):
                        emit(k, pair, f, pack(f, pair))


def finish_kernel(start, got, p_out, u_out, made, sems):
    tm, _ = block_index()
    outs = p_out, u_out

    @pl.when(tm == 0)
    def _():
        copies = [pltpu.make_async_copy(start.at[f], outs[f].at[0], sems.at[f]) for f in range(2)]
        for copy in copies:
            copy.start()
        for copy in copies:
            copy.wait()

    @pl.when(tm != 0)
    def _():
        copies = []
        for f in range(2):
            for rp in range(2):
                for b in range(4):
                    parts = transpose_lanes([got[MEMBER[8 * b + j], f, rp] for j in range(8)])
                    for g in range(4):
                        for rr in range(2):
                            at = slice(8 * g, 8 * g + 8), slice(128 * b, 128 * b + 128)
                            made[f, 2 * rp + rr, at[0], at[1]] = parts[2 * g + rr]
                rows = pl.ds(2 * rp, 2)
                copy = pltpu.make_async_copy(
                    made.at[f, rows], outs[f].at[0, rows], sems.at[2 * f + rp]
                )
                copy.start()
                copies.append(copy)
        for copy in copies:
            copy.wait()


VMEM = pl.BlockSpec(memory_space=pltpu.VMEM)
ANY = pl.BlockSpec(memory_space=pl.ANY)


def call(kernel, outs, args, scratch=(), specs=None, grant=40, out_spec=None, cost=8):
    shapes = [jax.ShapeDtypeStruct(s, jnp.float32) for s in outs]
    return pl.pallas_call(
        kernel,
        out_shape=shapes if len(shapes) > 1 else shapes[0],
        in_specs=specs or [VMEM] * len(args),
        out_specs=[out_spec or VMEM] * len(shapes) if len(shapes) > 1 else out_spec or VMEM,
        scratch_shapes=[pltpu.VMEM(s, jnp.float32) if isinstance(s, tuple) else s for s in scratch],
        cost_estimate=pl.CostEstimate(flops=8, bytes_accessed=cost, transcendentals=0),
        compiler_params=pltpu.CompilerParams(vmem_limit_bytes=grant * 1024 * 1024),
    )(*args)


def exchange(payload, axis, pairs):
    odd, even = payload
    got_odd = lax.ppermute(odd, axis, pairs(1))
    got_even = lax.ppermute(even, axis, pairs(0))
    return got_odd, got_even


def local(phase_guess, solute_guess, solute_start, nuclei):
    start = call(
        start_kernel,
        [(2, 4, 32, 512)],
        [nuclei.T, phase_guess, solute_guess, solute_start],
        scratch=[pltpu.SMEM((3, 8), jnp.int32), (2, 4, 32, 512), pltpu.SemaphoreType.DMA((9,))],
        out_spec=ANY,
        specs=[ANY] * 4,
        grant=60,
    )
    even = lax.ppermute(start, "space", space_pairs(0))
    odd = lax.ppermute(start, "space", space_pairs(1))
    staged = call(
        stage_kernel,
        [(2, 4, 32, 512)],
        [start],
        scratch=[pltpu.SemaphoreType.DMA],
        specs=[ANY],
        cost=4 * 10**6,
    )
    packed = call(
        relax_kernel,
        [(32, 2, 2, 8, 128)],
        [staged, odd, even],
        scratch=[(2, 12, 48, 512), (2, 12, 48, 512), (2, 4, 32, 512)],
    )
    own = lax.all_to_all(packed, AXES, 0, 0, tiled=True, axis_index_groups=PLANE_GROUPS)
    blank = [(16, 2, 2, 8, 128), (2, 8, 8, 128)]
    shapes = [(4 * blocks, 2, 2, 8, 128) for blocks in (2, 1, 4)]
    near, middle, far, once, *blank = pl.pallas_call(
        cut_kernel,
        out_shape=[jax.ShapeDtypeStruct(s, jnp.float32) for s in shapes]
        + [jax.ShapeDtypeStruct((1,), jnp.int32)]
        + [jax.ShapeDtypeStruct(s, jnp.float32) for s in blank],
        in_specs=[VMEM],
        out_specs=[VMEM, VMEM, VMEM, pl.BlockSpec(memory_space=pltpu.SMEM), ANY, ANY],
        compiler_params=pltpu.CompilerParams(vmem_limit_bytes=40 * 1024 * 1024),
    )(own)
    near = lax.ppermute(near, "tm", ACROSS)
    middle = lax.ppermute(middle, "tm", ACROSS)

    def lanes(phase, known):
        edges = call(
            lambda *refs: lanes_kernel(phase, *refs), [(4 * phase.steps, 2, 8, 128)] * 2, known
        )
        return exchange(edges, AXES, lane_pairs)

    def advance(phase, known, before=(), after=()):
        edges = call(
            lambda *refs: edges_kernel(phase, *refs[len(after) :]),
            [(phase.halo_at[-1], 2, 8, 128)] * 2,
            [*after, *known],
            specs=[ANY] * len(after) + [VMEM] * len(known),
        )
        return call(
            lambda *refs: chain_kernel(phase, *refs),
            [(32, 2, 2, 8, 128)] if phase.index else [(16, 2, 2, 8, 128), (2, 8, 8, 128)],
            [*known, *exchange(edges, AXES, row_pairs), *before],
            scratch=[(2, 2, 32, 8, 128), (phase.steps, 2, 32, 8, 128)],
        )

    known = [own, jnp.concatenate([near, middle])]
    far, _ = lax.optimization_barrier((far, near))
    crossed = lax.ppermute(far, "tm", ACROSS)
    known += lanes(PHASES[0], known)
    before, first = lax.fori_loop(
        0, once[0], lambda i, state: tuple(advance(PHASES[0], known, (), state[1:])), tuple(blank)
    )
    known = [own, crossed, first]
    known += lanes(PHASES[1], known)
    got = advance(PHASES[1], known, [before])
    back = lax.all_to_all(got, AXES, 0, 0, tiled=True, axis_index_groups=PLANE_GROUPS)
    return call(
        finish_kernel,
        [(1, 4, 32, 512)] * 2,
        [start, back],
        scratch=[(2, 4, 32, 512), pltpu.SemaphoreType.DMA((4,))],
        specs=[ANY, VMEM],
        out_spec=ANY,
    )


def solution(mesh):
    return jax.shard_map(
        lambda *args: tuple(local(*args)),
        mesh=mesh,
        in_specs=(
            P("tm", "space", None, None),
            P("tm", "space", None, None),
            P("space", None, None),
            P(),
        ),
        out_specs=(P("tm", "space", None, None), P("tm", "space", None, None)),
        check_vma=False,
    )
```
